128 devices in a mesh: blk: 32 (over z, y_hi, x), slab: 4 (over y_lo, core).
Axes of the slice: x: 4, y: 4 (y_hi: 2, y_lo: 2; y = y_hi * 2 + y_lo), z: 4, core: 2. Of those that a mesh axis runs over, the one named last changes fastest.
Arguments:
- priv_coeff: bfloat16 [32768, 16384], P('blk', 'slab'), may hold values from -0.046875 to 0.046875
- priv_var: float32 [32, 16384], P('blk', 'slab'), may hold values from 0.2 to 5
- shared_coeff: bfloat16 [32768, 1024], P('blk', 'slab'), may hold values from -0.09375 to 0.09375
- shared_var: float32 [32, 1024], P('blk', 'slab'), may hold values from 0.2 to 5
- partners: int32 [32, 2], replicated, may hold values from -1 to 30, as said below
Outputs:
- diag: float32 [32, 1024, 1024], P('blk', 'slab')
- tiles: float32 [32, 1024, 2, 1024], P('blk', 'slab')
- panel0: float32 [32768, 1024], P(('blk', 'slab'))
- panel1: float32 [32768, 1024], P(('blk', 'slab'))
The draws below stay inside these ranges and needn't reach their ends.
Inputs may be any that keep to these rules, and one draw needn't show every extreme that they name: `partners`: in every round the blocks are matched in pairs: each block is in exactly one pair of that round, and no two rounds pair the same two blocks. In each pair the larger-numbered block holds the other's number and the smaller holds -1. Blocks 32 - 1 and 30 are paired in one of the rounds.
All inputs are finite; a program needn't handle non-finite values.
Results may differ from the reference program's by a relative error of at most 0.004.
Values may be sent and summed in bfloat16 or wider, within the bound.
No kernel may reach another device: no remote copies, remote signals or barrier semaphores. Data moves between devices by JAX's collectives and lax.ppermute only.
A program may use at most 128 MiB of HBM per device.

```python
import math
import jax
import jax.numpy as jnp
from jax import lax

ROWS = 1024
SLOT = 128
PRIV_DEV = 32
ROUNDS = 2
BLOCKS = 32
N_SLAB = 4


def draw_partners(key, part):
    key = jax.random.fold_in(key, 7)
    key_perm, key_round = jax.random.split(key)
    chosen = jax.random.permutation(key_round, BLOCKS - 1)[:ROUNDS].astype(jnp.int32)
    rest_order = jax.random.permutation(key_perm, BLOCKS - 2).astype(jnp.int32)
    head_pos = jnp.arange(BLOCKS - 1, dtype=jnp.int32)
    first_spot = chosen[0]
    source_pos = jnp.clip(head_pos - (head_pos > first_spot).astype(jnp.int32), 0, BLOCKS - 3)
    head_labels = jnp.where(head_pos == first_spot, BLOCKS - 2, rest_order[source_pos])
    labels_of = jnp.concatenate([head_labels, jnp.full((1,), BLOCKS - 1, jnp.int32)]).astype(jnp.int32)
    places = jnp.argsort(labels_of, stable=True).astype(jnp.int32)
    spot_pos = places[:, None]
    round_ids = chosen[None, :]
    last_pos = BLOCKS - 1
    mirror = jnp.mod(2 * round_ids - spot_pos, last_pos)
    mate_spot = jnp.where(spot_pos == last_pos, round_ids, jnp.where(spot_pos == round_ids, last_pos, mirror))
    mate_ids = labels_of[mate_spot]
    block_ids = jnp.arange(BLOCKS, dtype=jnp.int32)[:, None]
    return jnp.where(mate_ids < block_ids, mate_ids, -1).astype(jnp.int32)


def levels(rng, extent, cuts, least, high):
    gain = 1.0
    for position, blocks in cuts:
        steps = jax.random.uniform(jax.random.fold_in(jax.random.fold_in(rng, 6), position), (blocks,), jnp.float32, least / len(cuts), high / len(cuts))
        gain = gain * jnp.repeat(jnp.exp(steps), extent[position] // blocks).reshape((-1,) + (1,) * (len(extent) - 1 - position))
    return gain


def centred(stream_key, shape, deviation, most, cuts=(), kind=jnp.bfloat16):
    gain = levels(stream_key, shape, cuts, -0.22, 0.18) if cuts else 1.0
    array = jax.random.normal(stream_key, shape, jnp.float32) * deviation * gain
    return jnp.minimum(jnp.maximum(array, -most), most).astype(kind)


def setup_inputs(seed: int = 0) -> dict:
    seeds = jax.random.split(jax.random.key(seed), 6)
    return {
        "priv_coeff": centred(seeds[0], (BLOCKS * ROWS, N_SLAB * PRIV_DEV * SLOT), (N_SLAB * SLOT * (PRIV_DEV + ROUNDS)) ** -0.5, 0.046875, ((0, 32), (1, 4))),
        "priv_var": jnp.clip(jnp.exp(math.log(5.0) - 3.218876 * jax.random.uniform(seeds[1], (BLOCKS, N_SLAB * PRIV_DEV * SLOT), jnp.float32) ** levels(seeds[1], (BLOCKS, N_SLAB * PRIV_DEV * SLOT), ((0, 32), (1, 4)), -0.2, 0.2)), 0.2, 5.0),
        "shared_coeff": centred(seeds[2], (BLOCKS * ROWS, N_SLAB * ROUNDS * SLOT), (N_SLAB * SLOT * (PRIV_DEV + ROUNDS) // 4) ** -0.5, 0.09375, ((0, 32), (1, 4))),
        "shared_var": jnp.clip(jnp.exp(math.log(5.0) - 3.218876 * jax.random.uniform(seeds[3], (BLOCKS, N_SLAB * ROUNDS * SLOT), jnp.float32) ** levels(seeds[3], (BLOCKS, N_SLAB * ROUNDS * SLOT), ((0, 32), (1, 4)), -0.2, 0.2)), 0.2, 5.0),
        "partners": draw_partners(jax.random.fold_in(seeds[5], 71), 0),
    }


def right_solve(factor, rows):
    return jax.scipy.linalg.solve_triangular(factor, rows.T, lower=True).T

def exact_nt(left, right):
    return jnp.dot(left.astype(jnp.float32), right.T.astype(jnp.float32), precision=lax.Precision.HIGHEST, preferred_element_type=jnp.float32)

def reference(priv_coeff, priv_var, shared_coeff, shared_var, partners):
    labels = jnp.arange(BLOCKS, dtype=jnp.int32)
    larger = partners >= 0
    named_by = (partners[:, :, None] == labels[None, None, :]).astype(jnp.int32)
    smaller_of = jnp.sum(named_by * labels[:, None, None], axis=0)
    mate_ids = jnp.where(larger, partners, smaller_of.T).astype(jnp.int32)
    var_grid = shared_var.reshape(BLOCKS, N_SLAB, ROUNDS, SLOT)
    mate_cols = []
    for turn in range(ROUNDS):
        mate_cols.append(var_grid[mate_ids[:, turn], :, turn, :])
    mate_var = jnp.stack(mate_cols, axis=2)
    var_eff = jnp.where(larger[:, None, :, None], var_grid, mate_var).reshape(BLOCKS, -1)
    priv_blocks = priv_coeff.reshape(BLOCKS, ROWS, -1)
    shared_blocks = shared_coeff.reshape(BLOCKS, ROWS, -1)

    def block_tiles(index):
        own_priv = lax.dynamic_index_in_dim(priv_blocks, index, 0, False).astype(jnp.float32)
        own_shared = lax.dynamic_index_in_dim(shared_blocks, index, 0, False).astype(jnp.float32)
        priv_scale = lax.dynamic_index_in_dim(priv_var, index, 0, False)
        shared_scale = lax.dynamic_index_in_dim(var_eff, index, 0, False)
        weighted_priv = own_priv * priv_scale
        weighted_shared = own_shared * shared_scale
        diag_tile = exact_nt(weighted_priv, own_priv)
        diag_tile = diag_tile + exact_nt(weighted_shared, own_shared)
        own_partners = lax.dynamic_index_in_dim(partners, index, 0, False)
        pair_tiles = []
        for turn in range(ROUNDS):
            other = jnp.maximum(own_partners[turn], 0)
            other_shared = lax.dynamic_index_in_dim(shared_blocks, other, 0, False).astype(jnp.float32)
            left_cols = weighted_shared.reshape(ROWS, N_SLAB, ROUNDS, SLOT)[:, :, turn, :].reshape(ROWS, -1)
            right_cols = other_shared.reshape(ROWS, N_SLAB, ROUNDS, SLOT)[:, :, turn, :].reshape(ROWS, -1)
            product = exact_nt(left_cols, right_cols)
            pair_tiles.append(jnp.where(own_partners[turn] >= 0, product, jnp.zeros_like(product)))
        return (diag_tile, jnp.stack(pair_tiles, axis=1))
    diag, tiles = lax.map(block_tiles, labels)
    first_factor = jnp.linalg.cholesky(diag[0])
    col_first = jnp.sum(jnp.where((partners == 0)[:, None, :, None], tiles, 0.0), axis=2).reshape(BLOCKS * ROWS, ROWS)
    solved = right_solve(first_factor, col_first)
    panel0 = jnp.concatenate([first_factor, solved[ROWS:]], axis=0)
    left_rows = panel0[ROWS:2 * ROWS]
    second_factor = jnp.linalg.cholesky(diag[1] - exact_nt(left_rows, left_rows))
    col_second = jnp.sum(jnp.where((partners == 1)[:, None, :, None], tiles, 0.0), axis=2).reshape(BLOCKS * ROWS, ROWS)
    rest = col_second - exact_nt(panel0, left_rows)
    solved_second = right_solve(second_factor, rest)
    panel1 = jnp.concatenate([jnp.zeros((ROWS, ROWS), jnp.float32), second_factor, solved_second[2 * ROWS:]], axis=0)
    return (diag, tiles, panel0, panel1)
```

```python
import functools

import jax
import jax.numpy as jnp
from jax import lax
from jax.experimental import pallas as pl
from jax.experimental.pallas import tpu as pltpu
from jax.sharding import PartitionSpec as P

SLOT = 128
NB = 128
SUB = 8
BIG = 256
DEPTH = 512
DIAG_SCALE = 256.0
SOLVE_SCALE = 4096.0
SMEM = pl.BlockSpec(memory_space=pltpu.SMEM)
VMEM = pl.BlockSpec(memory_space=pltpu.VMEM)
NT = (((1,), (1,)), ((), ()))
NN = (((1,), (0,)), ((), ()))


def params():
    return pltpu.CompilerParams(vmem_limit_bytes=48 * 1024 * 1024)


def tri(i, j):
    return i * (i + 1) // 2 + j


def halves(x):
    hi = x.astype(jnp.bfloat16)
    return hi, (x - hi.astype(jnp.float32)).astype(jnp.bfloat16)


def mul(left, right, dims):
    return lax.dot_general(left, right, dims, preferred_element_type=jnp.float32)


def mul3(left, right, dims=NT):
    (lh, ll), (rh, rl) = left, right
    return mul(lh, rh, dims) + (mul(lh, rl, dims) + mul(ll, rh, dims))


def partial_kernel(core_ref, priv_ref, var_ref, shared_ref, scale_ref, out_ref):
    per_half = out_ref.shape[1]
    big = out_ref.shape[2]
    tiles = [(i, j) for i in range(priv_ref.shape[0] // big) for j in range(i + 1)]

    def add(coeff, scale, first):
        weighted = (coeff.astype(jnp.float32) * scale).astype(jnp.bfloat16)
        for t, (i, j) in enumerate(tiles):
            part = mul(weighted[big * i : big * i + big], coeff[big * j : big * j + big], NT)
            spot = (t // per_half) ^ core_ref[0]
            if first:
                out_ref[spot, t % per_half] = part
            else:
                out_ref[spot, t % per_half] = out_ref[spot, t % per_half] + part

    @pl.when(pl.program_id(0) == 0)
    def _():
        add(shared_ref[...], scale_ref[...], True)

    add(priv_ref[...], var_ref[...], False)


def partial_diag(core, priv, var, shared, scale):
    rows, cells = priv.shape
    depth = min(DEPTH, cells)
    big = min(BIG, rows // 4)
    per_half = (rows // big) * (rows // big + 1) // 4
    return pl.pallas_call(
        partial_kernel,
        out_shape=jax.ShapeDtypeStruct((2, per_half, big, big), jnp.float32),
        grid=(cells // depth,),
        in_specs=[
            SMEM,
            pl.BlockSpec((rows, depth), lambda k: (0, k)),
            pl.BlockSpec((1, depth), lambda k: (0, k)),
            pl.BlockSpec(shared.shape, lambda k: (0, 0)),
            pl.BlockSpec(scale.shape, lambda k: (0, 0)),
        ],
        out_specs=pl.BlockSpec((2, per_half, big, big), lambda k: (0, 0, 0, 0)),
        compiler_params=params(),
        cost_estimate=pl.CostEstimate(
            flops=rows * rows * cells * 5 // 4, bytes_accessed=rows * cells * 2, transcendentals=0
        ),
        name="partial_diag",
    )(core, priv, var, shared, scale)


def row_bcast(x, j):
    return jnp.broadcast_to(x[j:j+1, :], (SUB, NB))

def col_bcast(x, c):
    return jnp.broadcast_to(x[:, c:c+1], (SUB, NB))

def factor_tile(tile):
    groups = NB // SUB
    sub = lax.broadcasted_iota(jnp.int32, (SUB, NB), 0)
    lane = lax.broadcasted_iota(jnp.int32, (SUB, NB), 1)
    W = [tile[SUB*g:SUB*g+SUB, :] for g in range(groups)]
    V = [(lane == sub + SUB*g).astype(jnp.float32) for g in range(groups)]
    ups, invs = [], []
    dcol = [col_bcast(W[0], j) for j in range(SUB)]
    for g in range(groups):
        icol = [(sub == j).astype(jnp.float32) for j in range(SUB)]
        for k in range(SUB):
            r = lax.rsqrt(row_bcast(dcol[k], k))
            lk = dcol[k] * r
            for j in range(k+1, SUB):
                dcol[j] = dcol[j] - lk * row_bcast(lk, j)
            below = jnp.where(sub > k, lk, 0.0)
            for j in range(k+1):
                a = row_bcast(icol[j], k) * r
                icol[j] = jnp.where(sub == k, a, icol[j] - below * a)
        R, S = W[g], V[g]
        U = icol[0] * row_bcast(R, 0)
        SV = icol[0] * row_bcast(S, 0)
        for j in range(1, SUB):
            U = U + icol[j] * row_bcast(R, j)
            SV = SV + icol[j] * row_bcast(S, j)
        U = jnp.where(lane >= sub + SUB*g, U, 0.0)
        ups.append(U); invs.append(SV)
        if g + 1 < groups:
            Rn, Vn = W[g+1], V[g+1]
            bc = [col_bcast(Rn, SUB*g+j) for j in range(SUB)]
            dn = [col_bcast(Rn, SUB*(g+1)+j) for j in range(SUB)]
            for k in range(SUB):
                lc = bc[0] * row_bcast(icol[0], k)
                for j in range(1, k+1):
                    lc = lc + bc[j] * row_bcast(icol[j], k)
                for j in range(SUB):
                    dn[j] = dn[j] - lc * row_bcast(lc, j)
                Rn = Rn - lc * row_bcast(U, k)
                Vn = Vn - lc * row_bcast(SV, k)
            W[g+1], V[g+1] = Rn, Vn
            dcol = dn
        if g + 2 < groups:
            uh = U.astype(jnp.bfloat16).astype(jnp.float32)
            ul = U - uh
            sh = SV.astype(jnp.bfloat16).astype(jnp.float32)
            sl = SV - sh
            zero = jnp.zeros((SUB, NB), jnp.float32)
            lhs = jnp.concatenate([uh, ul, uh, zero], 0).astype(jnp.bfloat16)
            rhs = jnp.concatenate([
                jnp.concatenate([uh, uh, ul, zero], 0),
                jnp.concatenate([sh, sh, sl, zero], 0)], 1).astype(jnp.bfloat16)
            upd = lax.dot_general(lhs, rhs, (((0,), (0,)), ((), ())), preferred_element_type=jnp.float32)
            for t in range(g+2, groups):
                W[t] = W[t] - upd[SUB*t:SUB*t+SUB, :NB]
                V[t] = V[t] - upd[SUB*t:SUB*t+SUB, NB:]
    return jnp.concatenate(ups, 0), jnp.concatenate(invs, 0)


def chol_kernel(core_ref, slab_ref, mine_ref, other_ref, ct_ref, lrow_ref, zt_ref, M):
    n = zt_ref.shape[1]
    cb = n // NB
    extra = ct_ref.shape[0]
    total = n + extra
    quarter = lrow_ref.shape[0]
    big = mine_ref.shape[1]
    nbig = n // big
    half = mine_ref.shape[0]
    per = big // NB
    is0 = core_ref[0] == 0
    for i in range(nbig):
        for j in range(i+1):
            t = tri(i, j)
            if t < half:
                x = jnp.where(is0, mine_ref[t], other_ref[t])
            else:
                x = jnp.where(is0, other_ref[t-half], mine_ref[t-half])
            for b in range(per):
                M[j*per+b, big*i:big*i+big, :] = x[:, NB*b:NB*b+NB]
    for q in range(cb):
        M[q, n:total, :] = ct_ref[:, NB*q:NB*q+NB]

    def step_rest(p, inv):
        inv_parts = halves(inv)
        lo = (p+1)*NB
        below = mul3(halves(M[p, lo:total, :]), inv_parts)
        M[p, lo:total, :] = below
        high, low = halves(below)
        q = p + 1
        while q < cb:
            w = 2 if q + 1 < cb else 1
            a = (q - p - 1)*NB
            acc = mul3((high[a:], low[a:]), (high[a:a+w*NB], low[a:a+w*NB]))
            for b in range(w):
                M[q+b, q*NB:total, :] = M[q+b, q*NB:total, :] - acc[:, b*NB:b*NB+NB]
            q += w

    def body(p, carry):
        rows = pl.ds(pl.multiple_of(p*NB, NB), NB)
        up, inv = factor_tile(M[p, rows, :])
        M[p, rows, :] = up.T
        for s in range(cb):
            @pl.when(p == s)
            def _():
                step_rest(s, inv)
        return carry
    lax.fori_loop(0, cb, body, 0)
    start = pl.multiple_of(slab_ref[0]*quarter, quarter)
    ids = lax.broadcasted_iota(jnp.int32, (quarter, NB), 0) + start
    for q in range(cb):
        lrow_ref[:, NB*q:NB*q+NB] = jnp.where(ids >= q*NB, M[q, pl.ds(start, quarter), :], 0.0)
        zt_ref[:, NB*q:NB*q+NB] = M[q, n:total, :]

def chol_solve(core, slab, mine, other, ct, quarter):
    n = ct.shape[1]
    extra = ct.shape[0]
    return pl.pallas_call(
        chol_kernel,
        out_shape=(jax.ShapeDtypeStruct((quarter, n), jnp.float32), jax.ShapeDtypeStruct((extra, n), jnp.float32)),
        in_specs=[SMEM, SMEM, VMEM, VMEM, VMEM],
        out_specs=(VMEM, VMEM),
        scratch_shapes=[pltpu.VMEM((n//NB, n+extra, NB), jnp.float32)],
        compiler_params=params(),
        cost_estimate=pl.CostEstimate(flops=40 * 10**9, bytes_accessed=8 * n * n, transcendentals=0),
        name="factor_solve",
    )(core, slab, mine, other, ct)


def unpack_kernel(core_ref, slab_ref, mine_ref, other_ref, out_ref):
    per_half, big = mine_ref.shape[0], mine_ref.shape[1]
    row = slab_ref[0]
    for t in range(out_ref.shape[1] // big):
        high, low = jnp.maximum(row, t), jnp.minimum(row, t)
        spot = high * (high + 1) // 2 + low
        upper = (spot >= per_half).astype(jnp.int32)
        slot = spot - upper * per_half
        tile = jnp.where(upper == core_ref[0], mine_ref[slot], other_ref[slot])
        out_ref[:, big * t : big * t + big] = jnp.where(row < t, tile.T, tile)


def unpack_rows(core, slab, mine, other, rows):
    return pl.pallas_call(
        unpack_kernel,
        out_shape=jax.ShapeDtypeStruct((mine.shape[1], rows), jnp.float32),
        in_specs=[SMEM, SMEM, VMEM, VMEM],
        out_specs=VMEM,
        compiler_params=params(),
        name="diag_rows",
    )(core, slab, mine, other)


def forward_kernel(source_ref, held_ref, out_ref):
    rounds = source_ref.shape[1]
    for block in range(out_ref.shape[0]):
        for turn in range(rounds):
            cells = slice(SLOT * turn, SLOT * turn + SLOT)
            out_ref[block, :, cells] = held_ref[source_ref[block, turn], :, cells]


def forward(source, held):
    return pl.pallas_call(
        forward_kernel,
        out_shape=jax.ShapeDtypeStruct(held.shape, held.dtype),
        in_specs=[SMEM, VMEM],
        out_specs=VMEM,
        compiler_params=params(),
        name="forward",
    )(source, held)


def tiles_kernel(own_ref, weights_ref, others_ref, out_ref):
    slabs, rows = weights_ref.shape[0], others_ref.shape[1]
    for turn in range(own_ref.shape[0]):
        cells = slice(SLOT * turn, SLOT * turn + SLOT)
        listed = own_ref[turn] >= 0
        weight = jnp.concatenate([weights_ref[s, :, cells] for s in range(slabs)], axis=1)
        other = jnp.concatenate([others_ref[s, :, cells] for s in range(slabs)], axis=1)
        high, low = halves(weight)
        tile = mul(high, other, NT) + mul(low, other, NT)
        out_ref[:, rows * turn : rows * turn + rows] = jnp.where(listed, tile, 0.0)


def pair_tiles(own_row, weights, others):
    quarter, rows = weights.shape[1], others.shape[1]
    rounds = own_row.shape[0]
    return pl.pallas_call(
        tiles_kernel,
        out_shape=jax.ShapeDtypeStruct((quarter, rounds * rows), jnp.float32),
        in_specs=[SMEM, VMEM, VMEM],
        out_specs=VMEM,
        compiler_params=params(),
        name="pair_tiles",
    )(own_row, weights, others)


def panels_kernel(block_ref, own_ref, weights_ref, high_ref, low_ref, factor_ref, zero_ref, one_ref):
    slabs = weights_ref.shape[0]
    first, second = 0.0, 0.0
    for turn in range(own_ref.shape[0]):
        cells = slice(SLOT * turn, SLOT * turn + SLOT)
        weight = jnp.concatenate([weights_ref[s, :, cells] for s in range(slabs)], axis=1)
        high = jnp.concatenate([high_ref[s, cells, :] for s in range(slabs)], axis=0)
        low = jnp.concatenate([low_ref[s, cells, :] for s in range(slabs)], axis=0)
        solved = mul3(halves(weight), (high, low), NN)
        first = first + jnp.where(own_ref[turn] == 0, solved, 0.0)
        second = second + jnp.where(own_ref[turn] == 1, solved, 0.0)
    zero_ref[...] = jnp.where(block_ref[0] == 0, factor_ref[...], first)
    one_ref[...] = jnp.where(block_ref[0] == 1, factor_ref[...], second)


def panels(block, own_row, weights, high, low, factor_rows):
    shape = jax.ShapeDtypeStruct(factor_rows.shape, jnp.float32)
    return pl.pallas_call(
        panels_kernel,
        out_shape=(shape, shape),
        in_specs=[SMEM, SMEM, VMEM, VMEM, VMEM, VMEM],
        out_specs=(VMEM, VMEM),
        compiler_params=params(),
        name="panels",
    )(block, own_row, weights, high, low, factor_rows)


def spread(array, axis, root):
    mine = lax.axis_index(axis) == root
    return lax.psum(jnp.where(mine, array, jnp.zeros_like(array)), axis)


def exact_nt(left, right):
    return lax.dot_general(
        left, right, NT, precision=lax.Precision.HIGHEST, preferred_element_type=jnp.float32
    )


def coupled_panel(panel0, diag_part, tile_part, own_row, block_id, slab_id):
    quarter = panel0.shape[0]
    left_part, second_part = spread(panel0, "blk", 1), spread(diag_part, "blk", 1)
    left_full = lax.all_gather(left_part, "slab", axis=0, tiled=True)
    second_full = lax.all_gather(second_part, "slab", axis=0, tiled=True)
    second_factor = jnp.linalg.cholesky(second_full - exact_nt(left_full, left_full))
    col_second = jnp.sum(jnp.where((own_row == 1)[None, :, None], tile_part, 0.0), axis=1)
    rest = col_second - exact_nt(panel0, left_full)
    solved = jax.scipy.linalg.solve_triangular(second_factor, rest.T, lower=True).T
    second_rows = lax.dynamic_slice_in_dim(second_factor, slab_id * quarter, quarter, 0)
    return jnp.where(
        block_id == 0, jnp.zeros_like(solved), jnp.where(block_id == 1, second_rows, solved)
    )


def swap(array, step):
    return lax.ppermute(array, "slab", [(i, i ^ step) for i in range(lax.axis_size("slab"))])


def gather_slabs(array):
    near = jnp.stack([array, swap(array, 2)])
    far = swap(near, 1)
    return jnp.concatenate([near, far], axis=0)


SLAB_ORDER = (0, 2, 1, 3)


def on_device(priv_coeff, priv_var, shared_coeff, shared_var, partners):
    rows = priv_coeff.shape[0]
    blocks, rounds = partners.shape
    block_id = lax.axis_index("blk")
    slab_id = lax.axis_index("slab")
    slabs = lax.axis_size("slab")
    quarter = rows // slabs
    core = (slab_id % 2).astype(jnp.int32)[None]
    slab = slab_id.astype(jnp.int32)[None]
    block = block_id.astype(jnp.int32)[None]
    labels = jnp.arange(blocks, dtype=jnp.int32)
    own_row = lax.dynamic_index_in_dim(partners, block_id, 0, False)
    larger = own_row >= 0
    named_by = (partners == block_id).astype(jnp.int32)
    mate_ids = jnp.where(larger, own_row, jnp.sum(named_by * labels[:, None], axis=0))

    sent = jnp.broadcast_to(shared_var[None], (blocks,) + shared_var.shape)
    all_var = lax.all_to_all(sent, "blk", 0, 0, tiled=True).reshape(blocks, rounds, SLOT)
    chosen = jnp.where((labels[:, None] == mate_ids[None])[:, :, None], all_var, 0.0)
    mate_var = jnp.sum(chosen, axis=0)
    own_var = shared_var.reshape(rounds, SLOT)
    scale = jnp.where(larger[:, None], own_var, mate_var).reshape(1, rounds * SLOT)

    weighted = (shared_coeff.astype(jnp.float32) * shared_var).reshape(slabs, quarter, rounds * SLOT)
    parts = []
    for step in SLAB_ORDER:
        piece = lax.dynamic_index_in_dim(weighted, slab_id ^ step, 0, False)
        parts.append(swap(piece, step) if step else piece)
    weights = jnp.stack(parts)

    partial = partial_diag(core, priv_coeff, priv_var, shared_coeff, scale)
    up, down = DIAG_SCALE, 1.0 / DIAG_SCALE
    near = partial[0] + swap((partial[1] * up).astype(jnp.float16), 1).astype(jnp.float32) * down
    mine = near + swap((near * up).astype(jnp.float16), 2).astype(jnp.float32) * down
    other = swap(mine, 1)

    chunk = rows // blocks
    held = lax.all_to_all(shared_coeff.reshape(blocks, chunk, -1), "blk", 0, 0, tiled=True)
    passed = forward(jnp.maximum(partners, 0), held)
    mate_coeff = lax.all_to_all(passed, "blk", 0, 0, tiled=True).reshape(rows, -1)
    others = gather_slabs(mate_coeff)

    factor_rows, solved = chol_solve(core, slab, mine, other, shared_coeff.T.astype(jnp.float32), quarter)
    piece = solved.shape[0] // blocks
    out = (solved * SOLVE_SCALE).astype(jnp.float16).reshape(blocks, piece, rows)
    spread_out = lax.all_to_all(out, "blk", 0, 0, tiled=True)
    turn_here = block_id // (blocks // rounds)
    wanted = lax.dynamic_index_in_dim(partners, turn_here, 1, False)
    onward = jnp.where((wanted == 0)[:, None, None], spread_out[0][None], spread_out[1][None])
    arrived = lax.all_to_all(onward, "blk", 0, 0, tiled=True).reshape(solved.shape)
    every = gather_slabs(arrived).astype(jnp.float32) * (1.0 / SOLVE_SCALE)
    high = lax.reduce_precision(every, 8, 7)
    low = (every - high).astype(jnp.bfloat16)
    high = high.astype(jnp.bfloat16)

    diag_part = unpack_rows(core, slab, mine, other, rows)
    tile_part = pair_tiles(own_row, weights, others).reshape(quarter, rounds, rows)
    panel0, panel1 = panels(block, own_row, weights, high, low, factor_rows)
    coupled = jnp.any(lax.dynamic_index_in_dim(partners, 1, 0, False) == 0)
    panel1 = lax.cond(
        coupled,
        lambda: coupled_panel(panel0, diag_part, tile_part, own_row, block_id, slab_id),
        lambda: panel1,
    )
    return (diag_part[None], tile_part[None], panel0, panel1)


def solution(mesh):
    in_specs = (P("blk", "slab"), P("blk", "slab"), P("blk", "slab"), P("blk", "slab"), P())
    out_specs = (
        P("blk", "slab", None),
        P("blk", "slab", None, None),
        P(("blk", "slab"), None),
        P(("blk", "slab"), None),
    )
    return jax.shard_map(
        on_device, mesh=mesh, in_specs=in_specs, out_specs=out_specs, check_vma=False
    )
```

```python
import functools

import jax
import jax.numpy as jnp
from jax import lax
from jax.experimental import pallas as pl
from jax.experimental.pallas import tpu as pltpu
from jax.sharding import PartitionSpec as P

SLOT = 128
NB = 128
SUB = 8
BIG = 256
DEPTH = 1024
DIAG_SCALE = 256.0
SOLVE_SCALE = 4096.0
SMEM = pl.BlockSpec(memory_space=pltpu.SMEM)
VMEM = pl.BlockSpec(memory_space=pltpu.VMEM)
NT = (((1,), (1,)), ((), ()))
NN = (((1,), (0,)), ((), ()))


def params():
    return pltpu.CompilerParams(vmem_limit_bytes=48 * 1024 * 1024)


def tri(i, j):
    return i * (i + 1) // 2 + j


def halves(x):
    hi = x.astype(jnp.bfloat16)
    return hi, (x - hi.astype(jnp.float32)).astype(jnp.bfloat16)


def mul(left, right, dims):
    return lax.dot_general(left, right, dims, preferred_element_type=jnp.float32)


def mul3(left, right, dims=NT):
    (lh, ll), (rh, rl) = left, right
    return mul(lh, rh, dims) + (mul(lh, rl, dims) + mul(ll, rh, dims))


def partial_kernel(core_ref, coeff_ref, scale_ref, out_ref):
    per_half, big = out_ref.shape[1], out_ref.shape[2]
    coeff = coeff_ref[...]
    weighted = (coeff.astype(jnp.float32) * scale_ref[...]).astype(jnp.bfloat16)

    def add(first):
        for t, (i, j) in enumerate(packed(coeff.shape[0] // big)):
            part = mul(weighted[big * i : big * i + big], coeff[big * j : big * j + big], NT)
            spot = (t // per_half) ^ core_ref[0]
            if first:
                out_ref[spot, t % per_half] = part
            else:
                out_ref[spot, t % per_half] = out_ref[spot, t % per_half] + part

    @pl.when(pl.program_id(0) == 0)
    def _():
        add(True)

    @pl.when(pl.program_id(0) > 0)
    def _():
        add(False)


def packed(count):
    return [(i, j) for i in range(count) for j in range(i + 1)]


def partial_diag(core, coeff, scale):
    rows, cells = coeff.shape
    depth = min(DEPTH, cells)
    per_half = (rows // BIG) * (rows // BIG + 1) // 4
    shape = (2, per_half, BIG, BIG)
    return pl.pallas_call(
        partial_kernel,
        out_shape=jax.ShapeDtypeStruct(shape, jnp.float32),
        grid=(cells // depth,),
        in_specs=[
            SMEM,
            pl.BlockSpec((rows, depth), lambda k: (0, k)),
            pl.BlockSpec((1, depth), lambda k: (0, k)),
        ],
        out_specs=pl.BlockSpec(shape, lambda k: (0, 0, 0, 0)),
        compiler_params=params(),
        cost_estimate=pl.CostEstimate(
            flops=rows * rows * cells * 2, bytes_accessed=rows * cells * 2, transcendentals=0
        ),
        name="partial_diag",
    )(core, coeff, scale)


def shared_kernel(core_ref, coeff_ref, scale_ref, partial_ref, out_ref):
    per_half, big = out_ref.shape[1], out_ref.shape[2]
    coeff = coeff_ref[...]
    weighted = (coeff.astype(jnp.float32) * scale_ref[...]).astype(jnp.bfloat16)
    for t, (i, j) in enumerate(packed(coeff.shape[0] // big)):
        part = mul(weighted[big * i : big * i + big], coeff[big * j : big * j + big], NT)
        spot = (t // per_half) ^ core_ref[0]
        out_ref[spot, t % per_half] = partial_ref[spot, t % per_half] + part


def add_shared(core, coeff, scale, partial):
    return pl.pallas_call(
        shared_kernel,
        out_shape=jax.ShapeDtypeStruct(partial.shape, jnp.float32),
        in_specs=[SMEM, VMEM, VMEM, VMEM],
        out_specs=VMEM,
        input_output_aliases={3: 0},
        compiler_params=params(),
        name="add_shared",
    )(core, coeff, scale, partial)


def row_bcast(x, j):
    return jnp.broadcast_to(x[j:j+1, :], (SUB, NB))

def col_bcast(x, c):
    return jnp.broadcast_to(x[:, c:c+1], (SUB, NB))

def factor_tile(tile):
    groups = NB // SUB
    sub = lax.broadcasted_iota(jnp.int32, (SUB, NB), 0)
    lane = lax.broadcasted_iota(jnp.int32, (SUB, NB), 1)
    W = [tile[SUB*g:SUB*g+SUB, :] for g in range(groups)]
    V = [(lane == sub + SUB*g).astype(jnp.float32) for g in range(groups)]
    ups, invs = [], []
    dcol = [col_bcast(W[0], j) for j in range(SUB)]
    for g in range(groups):
        icol = [(sub == j).astype(jnp.float32) for j in range(SUB)]
        for k in range(SUB):
            r = lax.rsqrt(row_bcast(dcol[k], k))
            lk = dcol[k] * r
            for j in range(k+1, SUB):
                dcol[j] = dcol[j] - lk * row_bcast(lk, j)
            below = jnp.where(sub > k, lk, 0.0)
            for j in range(k+1):
                a = row_bcast(icol[j], k) * r
                icol[j] = jnp.where(sub == k, a, icol[j] - below * a)
        R, S = W[g], V[g]
        U = icol[0] * row_bcast(R, 0)
        SV = icol[0] * row_bcast(S, 0)
        for j in range(1, SUB):
            U = U + icol[j] * row_bcast(R, j)
            SV = SV + icol[j] * row_bcast(S, j)
        U = jnp.where(lane >= sub + SUB*g, U, 0.0)
        ups.append(U); invs.append(SV)
        if g + 1 < groups:
            Rn, Vn = W[g+1], V[g+1]
            bc = [col_bcast(Rn, SUB*g+j) for j in range(SUB)]
            dn = [col_bcast(Rn, SUB*(g+1)+j) for j in range(SUB)]
            for k in range(SUB):
                lc = bc[0] * row_bcast(icol[0], k)
                for j in range(1, k+1):
                    lc = lc + bc[j] * row_bcast(icol[j], k)
                for j in range(SUB):
                    dn[j] = dn[j] - lc * row_bcast(lc, j)
                Rn = Rn - lc * row_bcast(U, k)
                Vn = Vn - lc * row_bcast(SV, k)
            W[g+1], V[g+1] = Rn, Vn
            dcol = dn
        if g + 2 < groups:
            uh = U.astype(jnp.bfloat16).astype(jnp.float32)
            ul = U - uh
            sh = SV.astype(jnp.bfloat16).astype(jnp.float32)
            sl = SV - sh
            zero = jnp.zeros((SUB, NB), jnp.float32)
            lhs = jnp.concatenate([uh, ul, uh, zero], 0).astype(jnp.bfloat16)
            rhs = jnp.concatenate([
                jnp.concatenate([uh, uh, ul, zero], 0),
                jnp.concatenate([sh, sh, sl, zero], 0)], 1).astype(jnp.bfloat16)
            upd = lax.dot_general(lhs, rhs, (((0,), (0,)), ((), ())), preferred_element_type=jnp.float32)
            for t in range(g+2, groups):
                W[t] = W[t] - upd[SUB*t:SUB*t+SUB, :NB]
                V[t] = V[t] - upd[SUB*t:SUB*t+SUB, NB:]
    return jnp.concatenate(ups, 0), jnp.concatenate(invs, 0)


def chol_kernel(core_ref, slab_ref, mine_ref, other_ref, ct_ref, lrow_ref, zt_ref, M):
    n = zt_ref.shape[1]
    cb = n // NB
    extra = ct_ref.shape[0]
    total = n + extra
    quarter = lrow_ref.shape[0]
    big = mine_ref.shape[1]
    nbig = n // big
    half = mine_ref.shape[0]
    per = big // NB
    is0 = core_ref[0] == 0
    for i in range(nbig):
        for j in range(i+1):
            t = tri(i, j)
            if t < half:
                x = jnp.where(is0, mine_ref[t], other_ref[t])
            else:
                x = jnp.where(is0, other_ref[t-half], mine_ref[t-half])
            for b in range(per):
                M[j*per+b, big*i:big*i+big, :] = x[:, NB*b:NB*b+NB]
    for q in range(cb):
        M[q, n:total, :] = ct_ref[:, NB*q:NB*q+NB]

    def step_rest(p, inv):
        inv_parts = halves(inv)
        lo = (p+1)*NB
        below = mul3(halves(M[p, lo:total, :]), inv_parts)
        M[p, lo:total, :] = below
        high, low = halves(below)
        q = p + 1
        while q < cb:
            w = 2 if q + 1 < cb else 1
            a = (q - p - 1)*NB
            acc = mul3((high[a:], low[a:]), (high[a:a+w*NB], low[a:a+w*NB]))
            for b in range(w):
                M[q+b, q*NB:total, :] = M[q+b, q*NB:total, :] - acc[:, b*NB:b*NB+NB]
            q += w

    def body(p, carry):
        rows = pl.ds(pl.multiple_of(p*NB, NB), NB)
        up, inv = factor_tile(M[p, rows, :])
        M[p, rows, :] = up.T
        for s in range(cb):
            @pl.when(p == s)
            def _():
                step_rest(s, inv)
        return carry
    lax.fori_loop(0, cb, body, 0)
    start = pl.multiple_of(slab_ref[0]*quarter, quarter)
    ids = lax.broadcasted_iota(jnp.int32, (quarter, NB), 0) + start
    for q in range(cb):
        lrow_ref[:, NB*q:NB*q+NB] = jnp.where(ids >= q*NB, M[q, pl.ds(start, quarter), :], 0.0)
        zt_ref[:, NB*q:NB*q+NB] = M[q, n:total, :]

def chol_solve(core, slab, mine, other, ct, quarter):
    n = ct.shape[1]
    extra = ct.shape[0]
    return pl.pallas_call(
        chol_kernel,
        out_shape=(jax.ShapeDtypeStruct((quarter, n), jnp.float32), jax.ShapeDtypeStruct((extra, n), jnp.float32)),
        in_specs=[SMEM, SMEM, VMEM, VMEM, VMEM],
        out_specs=(VMEM, VMEM),
        scratch_shapes=[pltpu.VMEM((n//NB, n+extra, NB), jnp.float32)],
        compiler_params=params(),
        cost_estimate=pl.CostEstimate(flops=40 * 10**9, bytes_accessed=8 * n * n, transcendentals=0),
        name="factor_solve",
    )(core, slab, mine, other, ct)


def unpack_kernel(core_ref, slab_ref, mine_ref, other_ref, out_ref):
    per_half, big = mine_ref.shape[0], mine_ref.shape[1]
    row = slab_ref[0]
    for t in range(out_ref.shape[1] // big):
        high, low = jnp.maximum(row, t), jnp.minimum(row, t)
        spot = high * (high + 1) // 2 + low
        upper = (spot >= per_half).astype(jnp.int32)
        slot = spot - upper * per_half
        tile = jnp.where(upper == core_ref[0], mine_ref[slot], other_ref[slot])
        out_ref[:, big * t : big * t + big] = jnp.where(row < t, tile.T, tile)


def unpack_rows(core, slab, mine, other, rows):
    return pl.pallas_call(
        unpack_kernel,
        out_shape=jax.ShapeDtypeStruct((mine.shape[1], rows), jnp.float32),
        in_specs=[SMEM, SMEM, VMEM, VMEM],
        out_specs=VMEM,
        compiler_params=params(),
        name="diag_rows",
    )(core, slab, mine, other)


def forward_kernel(source_ref, held_ref, out_ref):
    rounds = source_ref.shape[1]
    for block in range(out_ref.shape[0]):
        for turn in range(rounds):
            cells = slice(SLOT * turn, SLOT * turn + SLOT)
            out_ref[block, :, cells] = held_ref[source_ref[block, turn], :, cells]


def forward(source, held):
    return pl.pallas_call(
        forward_kernel,
        out_shape=jax.ShapeDtypeStruct(held.shape, held.dtype),
        in_specs=[SMEM, VMEM],
        out_specs=VMEM,
        compiler_params=params(),
        name="forward",
    )(source, held)


def row_weights(coeff_refs, var_refs, cells):
    pieces = [c[:, cells].astype(jnp.float32) * v[:, cells] for c, v in zip(coeff_refs, var_refs)]
    return halves(jnp.concatenate(pieces, axis=1))


def tiles_kernel(own_ref, *refs):
    coeff_refs, var_refs, other_refs, out_ref = refs[:4], refs[4:8], refs[8:12], refs[12]
    rows = other_refs[0].shape[0]
    for turn in range(own_ref.shape[0]):
        cells = slice(SLOT * turn, SLOT * turn + SLOT)
        high, low = row_weights(coeff_refs, var_refs, cells)
        other = jnp.concatenate([x[:, cells] for x in other_refs], axis=1)
        tile = mul(high, other, NT) + mul(low, other, NT)
        out_ref[:, rows * turn : rows * turn + rows] = jnp.where(own_ref[turn] >= 0, tile, 0.0)


def pair_tiles(own_row, coeffs, variances, others):
    quarter, rows = coeffs[0].shape[0], others[0].shape[0]
    rounds = own_row.shape[0]
    return pl.pallas_call(
        tiles_kernel,
        out_shape=jax.ShapeDtypeStruct((quarter, rounds * rows), jnp.float32),
        in_specs=[SMEM] + [VMEM] * 12,
        out_specs=VMEM,
        compiler_params=params(),
        cost_estimate=pl.CostEstimate(flops=3 * 10**9, bytes_accessed=5 * 10**6, transcendentals=0),
        name="pair_tiles",
    )(own_row, *coeffs, *variances, *others)


def solved_sum(own_ref, coeff_refs, var_refs, high_refs, low_refs):
    first, second = 0.0, 0.0
    for turn in range(own_ref.shape[0]):
        cells = slice(SLOT * turn, SLOT * turn + SLOT)
        high = jnp.concatenate([x[cells, :] for x in high_refs], axis=0)
        low = jnp.concatenate([x[cells, :] for x in low_refs], axis=0)
        solved = mul3(row_weights(coeff_refs, var_refs, cells), (high, low), NN)
        first = first + jnp.where(own_ref[turn] == 0, solved, 0.0)
        second = second + jnp.where(own_ref[turn] == 1, solved, 0.0)
    return first, second


def near_kernel(own_ref, *refs):
    zero_ref, one_ref = refs[8:]
    zero_ref[...], one_ref[...] = solved_sum(own_ref, refs[:2], refs[2:4], refs[4:6], refs[6:8])


def far_kernel(block_ref, own_ref, *refs):
    near_zero_ref, near_one_ref, factor_ref, zero_ref, one_ref = refs[8:]
    first, second = solved_sum(own_ref, refs[:2], refs[2:4], refs[4:6], refs[6:8])
    block = block_ref[0]
    zero_ref[...] = jnp.where(block == 0, factor_ref[...], near_zero_ref[...] + first)
    one_ref[...] = jnp.where(block == 1, factor_ref[...], near_one_ref[...] + second)


def near_panels(own_row, coeffs, variances, highs, lows):
    shape = jax.ShapeDtypeStruct((coeffs[0].shape[0], highs[0].shape[1]), jnp.float32)
    return pl.pallas_call(
        near_kernel,
        out_shape=(shape, shape),
        in_specs=[SMEM] + [VMEM] * 8,
        out_specs=(VMEM, VMEM),
        compiler_params=params(),
        cost_estimate=pl.CostEstimate(flops=3 * 10**9, bytes_accessed=5 * 10**6, transcendentals=0),
        name="near_panels",
    )(own_row, *coeffs, *variances, *highs, *lows)


def far_panels(block, own_row, coeffs, variances, highs, lows, near, factor_rows):
    shape = jax.ShapeDtypeStruct(factor_rows.shape, jnp.float32)
    return pl.pallas_call(
        far_kernel,
        out_shape=(shape, shape),
        in_specs=[SMEM, SMEM] + [VMEM] * 11,
        out_specs=(VMEM, VMEM),
        compiler_params=params(),
        name="far_panels",
    )(block, own_row, *coeffs, *variances, *highs, *lows, *near, factor_rows)


def spread(array, axis, root):
    mine = lax.axis_index(axis) == root
    return lax.psum(jnp.where(mine, array, jnp.zeros_like(array)), axis)


def exact_nt(left, right):
    return lax.dot_general(
        left, right, NT, precision=lax.Precision.HIGHEST, preferred_element_type=jnp.float32
    )


def coupled_panel(panel0, diag_part, tile_part, own_row, block_id, slab_id):
    quarter = panel0.shape[0]
    left_part, second_part = spread(panel0, "blk", 1), spread(diag_part, "blk", 1)
    left_full = lax.all_gather(left_part, "slab", axis=0, tiled=True)
    second_full = lax.all_gather(second_part, "slab", axis=0, tiled=True)
    second_factor = jnp.linalg.cholesky(second_full - exact_nt(left_full, left_full))
    col_second = jnp.sum(jnp.where((own_row == 1)[None, :, None], tile_part, 0.0), axis=1)
    rest = col_second - exact_nt(panel0, left_full)
    solved = jax.scipy.linalg.solve_triangular(second_factor, rest.T, lower=True).T
    second_rows = lax.dynamic_slice_in_dim(second_factor, slab_id * quarter, quarter, 0)
    return jnp.where(
        block_id == 0, jnp.zeros_like(solved), jnp.where(block_id == 1, second_rows, solved)
    )


def swap(array, step):
    return lax.ppermute(array, "slab", [(i, i ^ step) for i in range(lax.axis_size("slab"))])


def gather_slabs(array):
    across = swap(array, 2)
    return array, swap(array, 1), across, swap(across, 1)


def unscaled_halves(array):
    array = array.astype(jnp.float32) * (1.0 / SOLVE_SCALE)
    high = lax.reduce_precision(array, 8, 7)
    return high.astype(jnp.bfloat16), (array - high).astype(jnp.bfloat16)


def on_device(priv_coeff, priv_var, shared_coeff, shared_var, partners):
    rows = priv_coeff.shape[0]
    blocks, rounds = partners.shape
    block_id = lax.axis_index("blk")
    slab_id = lax.axis_index("slab")
    slabs = lax.axis_size("slab")
    quarter = rows // slabs
    core = (slab_id % 2).astype(jnp.int32)[None]
    slab = slab_id.astype(jnp.int32)[None]
    block = block_id.astype(jnp.int32)[None]
    labels = jnp.arange(blocks, dtype=jnp.int32)
    own_row = lax.dynamic_index_in_dim(partners, block_id, 0, False)
    larger = own_row >= 0
    named_by = (partners == block_id).astype(jnp.int32)
    mate_ids = jnp.where(larger, own_row, jnp.sum(named_by * labels[:, None], axis=0))

    sent = jnp.broadcast_to(shared_var[None], (blocks,) + shared_var.shape)
    all_var = lax.all_to_all(sent, "blk", 0, 0, tiled=True).reshape(blocks, rounds, SLOT)
    chosen = jnp.where((labels[:, None] == mate_ids[None])[:, :, None], all_var, 0.0)
    mate_var = jnp.sum(chosen, axis=0)
    own_var = shared_var.reshape(rounds, SLOT)
    scale = jnp.where(larger[:, None], own_var, mate_var).reshape(1, rounds * SLOT)

    partial = partial_diag(core, priv_coeff, priv_var)
    partial, scale, coeff = lax.optimization_barrier((partial, scale, shared_coeff))
    partial = add_shared(core, coeff, scale, partial)
    up, down = DIAG_SCALE, 1.0 / DIAG_SCALE
    near = partial[0] + swap((partial[1] * up).astype(jnp.float16), 1).astype(jnp.float32) * down
    mine = near + swap((near * up).astype(jnp.float16), 2).astype(jnp.float32) * down

    chunk = rows // blocks
    held = lax.all_to_all(coeff.reshape(blocks, chunk, -1), "blk", 0, 0, tiled=True)
    passed = forward(jnp.maximum(partners, 0), held)
    mate_coeff = lax.all_to_all(passed, "blk", 0, 0, tiled=True).reshape(rows, -1)

    mine, _ = lax.optimization_barrier((mine, passed))
    other = swap(mine, 1)
    turned = shared_coeff.T.astype(jnp.float32)
    factor_rows, solved = chol_solve(core, slab, mine, other, turned, quarter)
    piece = solved.shape[0] // blocks
    out = (solved * SOLVE_SCALE).astype(jnp.float16).reshape(blocks, piece, rows)
    spread_out = lax.all_to_all(out, "blk", 0, 0, tiled=True)
    turn_here = block_id // (blocks // rounds)
    wanted = lax.dynamic_index_in_dim(partners, turn_here, 1, False)
    onward = jnp.where((wanted == 0)[:, None, None], spread_out[0][None], spread_out[1][None])

    _, coeff, var, mate_coeff = lax.optimization_barrier((out, shared_coeff, shared_var, mate_coeff))
    coeffs = []
    for step in range(slabs):
        rows_there = lax.dynamic_slice_in_dim(coeff, (slab_id ^ step) * quarter, quarter, 0)
        coeffs.append(swap(rows_there, step) if step else rows_there)
    variances = gather_slabs(var)
    others = gather_slabs(mate_coeff)
    diag_part = unpack_rows(core, slab, mine, other, rows)
    onward, diag_part = lax.optimization_barrier((onward, diag_part))
    arrived = lax.all_to_all(onward, "blk", 0, 0, tiled=True).reshape(solved.shape)
    tile_part = pair_tiles(own_row, coeffs, variances, others).reshape(quarter, rounds, rows)
    arrived, tile_part = lax.optimization_barrier((arrived, tile_part))

    every = [unscaled_halves(x) for x in gather_slabs(arrived)]
    highs, lows = [h for h, _ in every], [l for _, l in every]
    close = near_panels(own_row, coeffs[:2], variances[:2], highs[:2], lows[:2])

    def apart():
        return far_panels(
            block, own_row, coeffs[2:], variances[2:], highs[2:], lows[2:], close, factor_rows
        )

    def coupled():
        panel0, _ = apart()
        return panel0, coupled_panel(panel0, diag_part, tile_part, own_row, block_id, slab_id)

    partners_of_one = lax.dynamic_index_in_dim(partners, 1, 0, False)
    panel0, panel1 = lax.cond(jnp.any(partners_of_one == 0), coupled, apart)
    return (diag_part[None], tile_part[None], panel0, panel1)


def solution(mesh):
    in_specs = (P("blk", "slab"), P("blk", "slab"), P("blk", "slab"), P("blk", "slab"), P())
    out_specs = (
        P("blk", "slab", None),
        P("blk", "slab", None, None),
        P(("blk", "slab"), None),
        P(("blk", "slab"), None),
    )
    return jax.shard_map(
        on_device, mesh=mesh, in_specs=in_specs, out_specs=out_specs, check_vma=False
    )
```

```python
import functools

import jax
import jax.numpy as jnp
from jax import lax
from jax.experimental import pallas as pl
from jax.experimental.pallas import tpu as pltpu
from jax.sharding import PartitionSpec as P

SLOT = 128
NB = 128
SUB = 8
BIG = 256
TRIPLE = 16
DEPTH = 1024
DIAG_SCALE = 256.0
SOLVE_SCALE = 4096.0
SMEM = pl.BlockSpec(memory_space=pltpu.SMEM)
VMEM = pl.BlockSpec(memory_space=pltpu.VMEM)
NT = (((1,), (1,)), ((), ()))
NN = (((1,), (0,)), ((), ()))


def params():
    return pltpu.CompilerParams(vmem_limit_bytes=48 * 1024 * 1024)


def tri(i, j):
    return i * (i + 1) // 2 + j


def halves(x):
    hi = x.astype(jnp.bfloat16)
    return hi, (x - hi.astype(jnp.float32)).astype(jnp.bfloat16)


def mul(left, right, dims):
    return lax.dot_general(left, right, dims, preferred_element_type=jnp.float32)


def mul3(left, right, dims=NT):
    (lh, ll), (rh, rl) = left, right
    return mul(lh, rh, dims) + (mul(lh, rl, dims) + mul(ll, rh, dims))


def partial_kernel(place_ref, coeff_ref, scale_ref, out_ref):
    per_half, big = out_ref.shape[1], out_ref.shape[2]
    coeff = coeff_ref[...]
    weighted = (coeff.astype(jnp.float32) * scale_ref[...]).astype(jnp.bfloat16)

    def add(first):
        for t, (i, j) in enumerate(packed(coeff.shape[0] // big)):
            part = mul(weighted[big * i : big * i + big], coeff[big * j : big * j + big], NT)
            spot = (t // per_half) ^ place_ref[2]
            if first:
                out_ref[spot, t % per_half] = part
            else:
                out_ref[spot, t % per_half] = out_ref[spot, t % per_half] + part

    @pl.when(pl.program_id(0) == 0)
    def _():
        add(True)

    @pl.when(pl.program_id(0) > 0)
    def _():
        add(False)


def packed(count):
    return [(i, j) for i in range(count) for j in range(i + 1)]


def partial_diag(place, coeff, scale):
    rows, cells = coeff.shape
    depth = min(DEPTH, cells)
    per_half = (rows // BIG) * (rows // BIG + 1) // 4
    shape = (2, per_half, BIG, BIG)
    return pl.pallas_call(
        partial_kernel,
        out_shape=jax.ShapeDtypeStruct(shape, jnp.float32),
        grid=(cells // depth,),
        in_specs=[
            SMEM,
            pl.BlockSpec((rows, depth), lambda k: (0, k)),
            pl.BlockSpec((1, depth), lambda k: (0, k)),
        ],
        out_specs=pl.BlockSpec(shape, lambda k: (0, 0, 0, 0)),
        compiler_params=params(),
        cost_estimate=pl.CostEstimate(
            flops=rows * rows * cells * 2, bytes_accessed=rows * cells * 2, transcendentals=0
        ),
        name="partial_diag",
    )(place, coeff, scale)


def triple_sum(rows):
    rows = rows.astype(jnp.float32)
    return rows[0:1] + rows[1:2] + rows[2:3]


def shared_kernel(place_ref, partners_ref, coeff_ref, own_ref, held_ref, partial_ref, out_ref):
    per_half, big = out_ref.shape[1], out_ref.shape[2]
    blocks, rounds = held_ref.shape[0], held_ref.shape[2] // SLOT
    block, core = place_ref[0], place_ref[2]
    scales = []
    for turn in range(rounds):
        cells = slice(SLOT * turn, SLOT * turn + SLOT)
        listed = partners_ref[turn, block]
        mate = jnp.int32(0)
        for other in range(blocks):
            mate = jnp.where(partners_ref[turn, other] == block, other, mate)
        theirs = triple_sum(held_ref[mate, held_ref.shape[1] - TRIPLE :, cells])
        scales.append(jnp.where(listed >= 0, own_ref[:, cells], theirs))
    scale = jnp.concatenate(scales, axis=1)
    coeff = coeff_ref[...]
    weighted = (coeff.astype(jnp.float32) * scale).astype(jnp.bfloat16)
    for t, (i, j) in enumerate(packed(coeff.shape[0] // big)):
        part = mul(weighted[big * i : big * i + big], coeff[big * j : big * j + big], NT)
        spot = (t // per_half) ^ core
        out_ref[spot, t % per_half] = partial_ref[spot, t % per_half] + part


def add_shared(place, partners, coeff, own_var, held, partial):
    return pl.pallas_call(
        shared_kernel,
        out_shape=jax.ShapeDtypeStruct(partial.shape, jnp.float32),
        in_specs=[SMEM, SMEM, VMEM, VMEM, VMEM, VMEM],
        out_specs=VMEM,
        input_output_aliases={5: 0},
        compiler_params=params(),
        name="add_shared",
    )(place, partners, coeff, own_var, held, partial)


def pack_kernel(place_ref, coeff_ref, var_ref, pieces_ref, *rows_refs):
    chunk = pieces_ref.shape[1] - TRIPLE
    quarter = rows_refs[0].shape[0] - TRIPLE
    var = var_ref[...]
    high = var.astype(jnp.bfloat16).astype(jnp.float32)
    middle = (var - high).astype(jnp.bfloat16).astype(jnp.float32)
    low = var - high - middle
    line = lax.broadcasted_iota(jnp.int32, (TRIPLE, var.shape[1]), 0)
    triple = jnp.where(line == 0, high, jnp.where(line == 1, middle, jnp.where(line == 2, low, 0.0)))
    triple = triple.astype(jnp.bfloat16)
    for block in range(pieces_ref.shape[0]):
        pieces_ref[block, :chunk] = coeff_ref[chunk * block : chunk * block + chunk]
        pieces_ref[block, chunk:] = triple
    for step, rows_ref in enumerate(rows_refs):
        start = pl.multiple_of((place_ref[1] ^ step) * quarter, quarter)
        rows_ref[:quarter] = coeff_ref[pl.ds(start, quarter)]
        rows_ref[quarter:] = triple


def pack(place, coeff, var, blocks, slabs):
    rows, cells = coeff.shape
    return pl.pallas_call(
        pack_kernel,
        out_shape=[jax.ShapeDtypeStruct((blocks, rows // blocks + TRIPLE, cells), coeff.dtype)]
        + [jax.ShapeDtypeStruct((rows // slabs + TRIPLE, cells), coeff.dtype)] * slabs,
        in_specs=[SMEM, VMEM, VMEM],
        out_specs=[VMEM] * (slabs + 1),
        compiler_params=params(),
        name="pack",
    )(place, coeff, var)


def row_bcast(x, j):
    return jnp.broadcast_to(x[j:j+1, :], (SUB, NB))

def col_bcast(x, c):
    return jnp.broadcast_to(x[:, c:c+1], (SUB, NB))

def factor_columns(columns, inverse):
    out = []
    for k in range(SUB):
        column = columns[0] * row_bcast(inverse[0], k)
        for j in range(1, k+1):
            column = column + columns[j] * row_bcast(inverse[j], k)
        out.append(column)
    return out

def factor_tile(tile):
    groups = NB // SUB
    sub = lax.broadcasted_iota(jnp.int32, (SUB, NB), 0)
    lane = lax.broadcasted_iota(jnp.int32, (SUB, NB), 1)
    W = [tile[SUB*g:SUB*g+SUB, :] for g in range(groups)]
    V = [(lane == sub + SUB*g).astype(jnp.float32) for g in range(groups)]
    ups, invs = [], []
    dcol = [col_bcast(W[0], j) for j in range(SUB)]
    left = [col_bcast(W[1], j) for j in range(SUB)]
    right = [col_bcast(W[1], SUB+j) for j in range(SUB)]
    for g in range(groups):
        icol = [(sub == j).astype(jnp.float32) for j in range(SUB)]
        for k in range(SUB):
            r = lax.rsqrt(row_bcast(dcol[k], k))
            lk = dcol[k] * r
            r2 = r * r
            for j in range(k+1, SUB):
                dcol[j] = dcol[j] - (dcol[k] * row_bcast(dcol[k], j)) * r2
            below = jnp.where(sub > k, lk, 0.0)
            for j in range(k+1):
                a = row_bcast(icol[j], k) * r
                icol[j] = jnp.where(sub == k, a, icol[j] - below * a)
        R, S = W[g], V[g]
        U = icol[0] * row_bcast(R, 0)
        SV = icol[0] * row_bcast(S, 0)
        for j in range(1, SUB):
            U = U + icol[j] * row_bcast(R, j)
            SV = SV + icol[j] * row_bcast(S, j)
        U = jnp.where(lane >= sub + SUB*g, U, 0.0)
        ups.append(U); invs.append(SV)
        if g + 1 == groups:
            break
        first = factor_columns(left, icol)
        dcol = right
        for k in range(SUB):
            for j in range(SUB):
                dcol[j] = dcol[j] - first[k] * row_bcast(first[k], j)
            W[g+1] = W[g+1] - first[k] * row_bcast(U, k)
            V[g+1] = V[g+1] - first[k] * row_bcast(SV, k)
        if g + 2 == groups:
            continue
        second = factor_columns([col_bcast(W[g+2], SUB*g+j) for j in range(SUB)], icol)
        left = [col_bcast(W[g+2], SUB*(g+1)+j) for j in range(SUB)]
        right = [col_bcast(W[g+2], SUB*(g+2)+j) for j in range(SUB)]
        for k in range(SUB):
            for j in range(SUB):
                left[j] = left[j] - second[k] * row_bcast(first[k], j)
                right[j] = right[j] - second[k] * row_bcast(second[k], j)
            W[g+2] = W[g+2] - second[k] * row_bcast(U, k)
            V[g+2] = V[g+2] - second[k] * row_bcast(SV, k)
        if g + 3 < groups:
            uh = U.astype(jnp.bfloat16).astype(jnp.float32)
            ul = U - uh
            sh = SV.astype(jnp.bfloat16).astype(jnp.float32)
            sl = SV - sh
            zero = jnp.zeros((SUB, NB), jnp.float32)
            lhs = jnp.concatenate([uh, ul, uh, zero], 0).astype(jnp.bfloat16)
            rhs = jnp.concatenate([
                jnp.concatenate([uh, uh, ul, zero], 0),
                jnp.concatenate([sh, sh, sl, zero], 0)], 1).astype(jnp.bfloat16)
            upd = lax.dot_general(lhs, rhs, (((0,), (0,)), ((), ())), preferred_element_type=jnp.float32)
            for t in range(g+3, groups):
                W[t] = W[t] - upd[SUB*t:SUB*t+SUB, :NB]
                V[t] = V[t] - upd[SUB*t:SUB*t+SUB, NB:]
    return jnp.concatenate(ups, 0), jnp.concatenate(invs, 0)


def chol_kernel(place_ref, mine_ref, other_ref, ct_ref, lrow_ref, zt_ref, M):
    n = zt_ref.shape[1]
    cb = n // NB
    extra = ct_ref.shape[0]
    total = n + extra
    quarter = lrow_ref.shape[0]
    big = mine_ref.shape[1]
    nbig = n // big
    half = mine_ref.shape[0]
    per = big // NB
    is0 = place_ref[2] == 0
    for i in range(nbig):
        for j in range(i+1):
            t = tri(i, j)
            if t < half:
                x = jnp.where(is0, mine_ref[t], other_ref[t])
            else:
                x = jnp.where(is0, other_ref[t-half], mine_ref[t-half])
            for b in range(per):
                M[j*per+b, big*i:big*i+big, :] = x[:, NB*b:NB*b+NB]
    for q in range(cb):
        M[q, n:total, :] = ct_ref[:, NB*q:NB*q+NB]

    def step_rest(p, inv):
        inv_parts = halves(inv)
        lo = (p+1)*NB
        below = mul3(halves(M[p, lo:total, :]), inv_parts)
        M[p, lo:total, :] = below
        high, low = halves(below)
        q = p + 1
        while q < cb:
            w = 2 if q + 1 < cb else 1
            a = (q - p - 1)*NB
            acc = mul3((high[a:], low[a:]), (high[a:a+w*NB], low[a:a+w*NB]))
            for b in range(w):
                M[q+b, q*NB:total, :] = M[q+b, q*NB:total, :] - acc[:, b*NB:b*NB+NB]
            q += w

    def body(p, carry):
        rows = pl.ds(pl.multiple_of(p*NB, NB), NB)
        up, inv = factor_tile(M[p, rows, :])
        M[p, rows, :] = up.T
        for s in range(cb):
            @pl.when(p == s)
            def _():
                step_rest(s, inv)
        return carry
    lax.fori_loop(0, cb, body, 0)
    start = pl.multiple_of(place_ref[1]*quarter, quarter)
    ids = lax.broadcasted_iota(jnp.int32, (quarter, NB), 0) + start
    for q in range(cb):
        lrow_ref[:, NB*q:NB*q+NB] = jnp.where(ids >= q*NB, M[q, pl.ds(start, quarter), :], 0.0)
        zt_ref[:, NB*q:NB*q+NB] = M[q, n:total, :]

def chol_solve(place, mine, other, ct, quarter):
    n = ct.shape[1]
    extra = ct.shape[0]
    return pl.pallas_call(
        chol_kernel,
        out_shape=(jax.ShapeDtypeStruct((quarter, n), jnp.float32), jax.ShapeDtypeStruct((extra, n), jnp.float32)),
        in_specs=[SMEM, VMEM, VMEM, VMEM],
        out_specs=(VMEM, VMEM),
        scratch_shapes=[pltpu.VMEM((n//NB, n+extra, NB), jnp.float32)],
        compiler_params=params(),
        cost_estimate=pl.CostEstimate(flops=40 * 10**9, bytes_accessed=8 * n * n, transcendentals=0),
        name="factor_solve",
    )(place, mine, other, ct)


def unpack_kernel(place_ref, mine_ref, other_ref, out_ref):
    per_half, big = mine_ref.shape[0], mine_ref.shape[1]
    row = place_ref[1]
    for t in range(out_ref.shape[1] // big):
        high, low = jnp.maximum(row, t), jnp.minimum(row, t)
        spot = high * (high + 1) // 2 + low
        upper = (spot >= per_half).astype(jnp.int32)
        slot = spot - upper * per_half
        tile = jnp.where(upper == place_ref[2], mine_ref[slot], other_ref[slot])
        out_ref[:, big * t : big * t + big] = jnp.where(row < t, tile.T, tile)


def unpack_rows(place, mine, other, rows):
    return pl.pallas_call(
        unpack_kernel,
        out_shape=jax.ShapeDtypeStruct((mine.shape[1], rows), jnp.float32),
        in_specs=[SMEM, VMEM, VMEM],
        out_specs=VMEM,
        compiler_params=params(),
        name="diag_rows",
    )(place, mine, other)


def forward_kernel(partners_ref, held_ref, out_ref):
    blocks, chunk, cells = out_ref.shape
    rounds = cells // SLOT
    for block in range(blocks):
        for turn in range(rounds):
            source = jnp.maximum(partners_ref[turn, block], 0)
            columns = slice(SLOT * turn, SLOT * turn + SLOT)
            out_ref[block, :, columns] = held_ref[source, :chunk, columns]


def forward(partners, held):
    return pl.pallas_call(
        forward_kernel,
        out_shape=jax.ShapeDtypeStruct((held.shape[0], held.shape[1] - TRIPLE, held.shape[2]), held.dtype),
        in_specs=[SMEM, VMEM],
        out_specs=VMEM,
        compiler_params=params(),
        name="forward",
    )(partners, held)


def row_weights(row_refs, cells):
    pieces = []
    for ref in row_refs:
        quarter = ref.shape[0] - TRIPLE
        pieces.append(ref[:quarter, cells].astype(jnp.float32) * triple_sum(ref[quarter:, cells]))
    return halves(jnp.concatenate(pieces, axis=1))


def tiles_kernel(place_ref, partners_ref, *refs):
    row_refs, other_refs, out_ref = refs[:4], refs[4:8], refs[8]
    rows, rounds = other_refs[0].shape[0], other_refs[0].shape[1] // SLOT
    for turn in range(rounds):
        cells = slice(SLOT * turn, SLOT * turn + SLOT)
        high, low = row_weights(row_refs, cells)
        other = jnp.concatenate([x[:, cells] for x in other_refs], axis=1)
        tile = mul(high, other, NT) + mul(low, other, NT)
        listed = partners_ref[turn, place_ref[0]] >= 0
        out_ref[:, rows * turn : rows * turn + rows] = jnp.where(listed, tile, 0.0)


def pair_tiles(place, partners, own_rows, others):
    quarter, (rows, cells) = own_rows[0].shape[0] - TRIPLE, others[0].shape
    return pl.pallas_call(
        tiles_kernel,
        out_shape=jax.ShapeDtypeStruct((quarter, cells // SLOT * rows), jnp.float32),
        in_specs=[SMEM, SMEM] + [VMEM] * 8,
        out_specs=VMEM,
        compiler_params=params(),
        cost_estimate=pl.CostEstimate(flops=3 * 10**9, bytes_accessed=5 * 10**6, transcendentals=0),
        name="pair_tiles",
    )(place, partners, *own_rows, *others)


def solved_sum(place_ref, partners_ref, row_refs, high_refs, low_refs):
    rounds = row_refs[0].shape[1] // SLOT
    first, second = 0.0, 0.0
    for turn in range(rounds):
        cells = slice(SLOT * turn, SLOT * turn + SLOT)
        high = jnp.concatenate([x[cells, :] for x in high_refs], axis=0)
        low = jnp.concatenate([x[cells, :] for x in low_refs], axis=0)
        solved = mul3(row_weights(row_refs, cells), (high, low), NN)
        listed = partners_ref[turn, place_ref[0]]
        first = first + jnp.where(listed == 0, solved, 0.0)
        second = second + jnp.where(listed == 1, solved, 0.0)
    return first, second


def near_kernel(place_ref, partners_ref, *refs):
    factor_ref, zero_ref, one_ref = refs[6:]
    first, second = solved_sum(place_ref, partners_ref, refs[:2], refs[2:4], refs[4:6])
    zero_ref[...] = jnp.where(place_ref[0] == 0, factor_ref[...], first)
    one_ref[...] = jnp.where(place_ref[0] == 1, factor_ref[...], second)


def far_kernel(place_ref, partners_ref, *refs):
    near_zero_ref, near_one_ref, zero_ref, one_ref = refs[6:]
    first, second = solved_sum(place_ref, partners_ref, refs[:2], refs[2:4], refs[4:6])
    zero_ref[...] = near_zero_ref[...] + jnp.where(place_ref[0] == 0, 0.0, first)
    one_ref[...] = near_one_ref[...] + jnp.where(place_ref[0] == 1, 0.0, second)


def chosen_sum(place_ref, partners_ref, row_refs, high_refs, low_refs):
    block = place_ref[0]
    later = partners_ref[1, block]
    is_later = jnp.logical_or(later == 0, later == 1)
    listed = jnp.where(is_later, later, partners_ref[0, block])
    pieces = []
    for ref in row_refs:
        quarter = ref.shape[0] - TRIPLE
        parts = []
        for turn in range(2):
            cells = slice(SLOT * turn, SLOT * turn + SLOT)
            parts.append(ref[:quarter, cells].astype(jnp.float32) * triple_sum(ref[quarter:, cells]))
        pieces.append(jnp.where(is_later, parts[1], parts[0]))
    weight = halves(jnp.concatenate(pieces, axis=1))
    high = jnp.concatenate([x[...] for x in high_refs], axis=0)
    low = jnp.concatenate([x[...] for x in low_refs], axis=0)
    solved = mul3(weight, (high, low), NN)
    return jnp.where(listed == 0, solved, 0.0), jnp.where(listed == 1, solved, 0.0)


def near_chosen_kernel(place_ref, partners_ref, *refs):
    factor_ref, zero_ref, one_ref = refs[6:]
    first, second = chosen_sum(place_ref, partners_ref, refs[:2], refs[2:4], refs[4:6])
    zero_ref[...] = jnp.where(place_ref[0] == 0, factor_ref[...], first)
    one_ref[...] = jnp.where(place_ref[0] == 1, factor_ref[...], second)


def far_chosen_kernel(place_ref, partners_ref, *refs):
    near_zero_ref, near_one_ref, zero_ref, one_ref = refs[6:]
    first, second = chosen_sum(place_ref, partners_ref, refs[:2], refs[2:4], refs[4:6])
    zero_ref[...] = near_zero_ref[...] + jnp.where(place_ref[0] == 0, 0.0, first)
    one_ref[...] = near_one_ref[...] + jnp.where(place_ref[0] == 1, 0.0, second)


def panels(kernel, place, partners, own_rows, highs, lows, more):
    shape = jax.ShapeDtypeStruct((own_rows[0].shape[0] - TRIPLE, highs[0].shape[1]), jnp.float32)
    return pl.pallas_call(
        kernel,
        out_shape=(shape, shape),
        in_specs=[SMEM, SMEM] + [VMEM] * (6 + len(more)),
        out_specs=(VMEM, VMEM),
        compiler_params=params(),
        cost_estimate=pl.CostEstimate(flops=3 * 10**9, bytes_accessed=5 * 10**6, transcendentals=0),
        name=kernel.__name__[:-7] + "_panels",
    )(place, partners, *own_rows, *highs, *lows, *more)


def spread(array, axis, root):
    mine = lax.axis_index(axis) == root
    return lax.psum(jnp.where(mine, array, jnp.zeros_like(array)), axis)


def exact_nt(left, right):
    return lax.dot_general(
        left, right, NT, precision=lax.Precision.HIGHEST, preferred_element_type=jnp.float32
    )


def coupled_panel(panel0, diag_part, tile_part, own_row, block_id, slab_id):
    quarter = panel0.shape[0]
    left_part, second_part = spread(panel0, "blk", 1), spread(diag_part, "blk", 1)
    left_full = lax.all_gather(left_part, "slab", axis=0, tiled=True)
    second_full = lax.all_gather(second_part, "slab", axis=0, tiled=True)
    second_factor = jnp.linalg.cholesky(second_full - exact_nt(left_full, left_full))
    col_second = jnp.sum(jnp.where((own_row == 1)[None, :, None], tile_part, 0.0), axis=1)
    rest = col_second - exact_nt(panel0, left_full)
    solved = jax.scipy.linalg.solve_triangular(second_factor, rest.T, lower=True).T
    second_rows = lax.dynamic_slice_in_dim(second_factor, slab_id * quarter, quarter, 0)
    return jnp.where(
        block_id == 0, jnp.zeros_like(solved), jnp.where(block_id == 1, second_rows, solved)
    )


def swap(array, step):
    return lax.ppermute(array, "slab", [(i, i ^ step) for i in range(lax.axis_size("slab"))])


def unscaled_halves(array):
    array = array.astype(jnp.float32) * (1.0 / SOLVE_SCALE)
    high = lax.reduce_precision(array, 8, 7)
    return high.astype(jnp.bfloat16), (array - high).astype(jnp.bfloat16)


def on_device(priv_coeff, priv_var, shared_coeff, shared_var, partners):
    rows = priv_coeff.shape[0]
    blocks, rounds = partners.shape
    block_id = lax.axis_index("blk").astype(jnp.int32)
    slab_id = lax.axis_index("slab").astype(jnp.int32)
    slabs = lax.axis_size("slab")
    quarter = rows // slabs
    place = jnp.stack([block_id, slab_id, slab_id % 2])
    table = partners.T

    pieces, *own_rows = pack(place, shared_coeff, shared_var, blocks, slabs)
    held = lax.all_to_all(pieces, "blk", 0, 0, tiled=True)
    own_rows = [swap(x, step) if step else x for step, x in enumerate(own_rows)]

    partial = partial_diag(place, priv_coeff, priv_var)
    partial, held, own_rows = lax.optimization_barrier((partial, held, own_rows))
    partial = add_shared(place, table, shared_coeff, shared_var, held, partial)
    up, down = DIAG_SCALE, 1.0 / DIAG_SCALE
    near = partial[0] + swap((partial[1] * up).astype(jnp.float16), 1).astype(jnp.float32) * down
    across = swap((near * up).astype(jnp.float16), 2)

    mate_coeff = lax.all_to_all(forward(table, held), "blk", 0, 0, tiled=True).reshape(rows, -1)
    across, mate_coeff = lax.optimization_barrier((across, mate_coeff))
    mine = near + across.astype(jnp.float32) * down

    from_zero, from_one = partners == 0, partners == 1
    one_each = jnp.logical_not(jnp.any(jnp.any(from_zero, axis=1) & jnp.any(from_one, axis=1)))
    is_coupled = jnp.any(from_zero[1])
    is_simple = one_each & jnp.logical_not(is_coupled)
    later = from_zero[:, 1] | from_one[:, 1]
    zero_later = jnp.where(later, from_zero[:, 1], from_zero[:, 0])
    choice = jnp.where(zero_later, 0, 2) + later.astype(jnp.int32)
    mine, choice, is_simple, is_coupled = lax.optimization_barrier((mine, choice, is_simple, is_coupled))

    other = swap(mine, 1)
    others = [swap(mate_coeff, step) if step else mate_coeff for step in (0, 1, 2)]
    cells = SLOT // blocks
    turned = shared_coeff.reshape(rows, rounds, blocks, cells).transpose(2, 1, 3, 0)
    turned = turned.reshape(rounds * SLOT, rows).astype(jnp.float32)
    factor_rows, solved = chol_solve(place, mine, other, turned, quarter)
    out = (solved * SOLVE_SCALE).astype(jnp.float16).reshape(blocks, rounds * cells, rows)
    spread_out = lax.all_to_all(out, "blk", 0, 0, tiled=True)
    diag_part = unpack_rows(place, mine, other, rows)
    _, others = lax.optimization_barrier((out, others))
    others = others + [swap(others[2], 1)]
    spread_out, diag_part = lax.optimization_barrier((spread_out, diag_part))

    def deliver(onward):
        arrived = lax.all_to_all(onward, "blk", 0, 0, tiled=True)
        tile_part = pair_tiles(place, table, own_rows, others).reshape(quarter, rounds, rows)
        return lax.optimization_barrier((arrived, tile_part))

    def finish(arrived, near, far):
        beside, across = swap(arrived, 1), swap(arrived, 2)
        highs, lows = zip(*[unscaled_halves(x) for x in (arrived, beside)])
        close = panels(near, place, table, own_rows[:2], highs, lows, (factor_rows,))
        across, close = lax.optimization_barrier((across, close))
        highs, lows = zip(*[unscaled_halves(x) for x in (across, swap(across, 1))])
        return panels(far, place, table, own_rows[2:], highs, lows, close)

    def simple():
        held = [spread_out[source, cells * turn : cells * turn + cells] for source in (0, 1) for turn in (0, 1)]
        onward = jnp.broadcast_to(held[0][None], (blocks, cells, rows))
        for place_of, piece in enumerate(held[1:], 1):
            onward = jnp.where((choice == place_of)[:, None, None], piece[None], onward)
        arrived, tile_part = deliver(onward)
        panel0, panel1 = finish(arrived.reshape(SLOT, rows), near_chosen_kernel, far_chosen_kernel)
        return tile_part, panel0, panel1

    def general():
        wanted = jnp.repeat(from_zero, cells, axis=1)[:, :, None]
        arrived, tile_part = deliver(jnp.where(wanted, spread_out[0][None], spread_out[1][None]))
        arrived = arrived.reshape(blocks, rounds, cells, rows).transpose(1, 0, 2, 3)
        panel0, panel1 = finish(arrived.reshape(solved.shape), near_kernel, far_kernel)
        own_row = lax.dynamic_index_in_dim(partners, block_id, 0, False)
        panel1 = lax.cond(
            is_coupled,
            lambda: coupled_panel(panel0, diag_part, tile_part, own_row, block_id, slab_id),
            lambda: panel1,
        )
        return tile_part, panel0, panel1

    tile_part, panel0, panel1 = lax.cond(is_simple, simple, general)
    return (diag_part[None], tile_part[None], panel0, panel1)


def solution(mesh):
    in_specs = (P("blk", "slab"), P("blk", "slab"), P("blk", "slab"), P("blk", "slab"), P())
    out_specs = (
        P("blk", "slab", None),
        P("blk", "slab", None, None),
        P(("blk", "slab"), None),
        P(("blk", "slab"), None),
    )
    return jax.shard_map(
        on_device, mesh=mesh, in_specs=in_specs, out_specs=out_specs, check_vma=False
    )
```

```python
import functools

import jax
import jax.numpy as jnp
from jax import lax
from jax.experimental import pallas as pl
from jax.experimental.pallas import tpu as pltpu
from jax.sharding import PartitionSpec as P

SLOT = 128
NB = 128
SUB = 8
BIG = 256
TRIPLE = 16
DEPTH = 1024
DIAG_SCALE = 256.0
SOLVE_SCALE = 4096.0
SMEM = pl.BlockSpec(memory_space=pltpu.SMEM)
VMEM = pl.BlockSpec(memory_space=pltpu.VMEM)
NT = (((1,), (1,)), ((), ()))
NN = (((1,), (0,)), ((), ()))


def params():
    return pltpu.CompilerParams(vmem_limit_bytes=48 * 1024 * 1024)


def tri(i, j):
    return i * (i + 1) // 2 + j


def halves(x):
    hi = x.astype(jnp.bfloat16)
    return hi, (x - hi.astype(jnp.float32)).astype(jnp.bfloat16)


def mul(left, right, dims):
    return lax.dot_general(left, right, dims, preferred_element_type=jnp.float32)


def mul3(left, right, dims=NT):
    (lh, ll), (rh, rl) = left, right
    return mul(lh, rh, dims) + (mul(lh, rl, dims) + mul(ll, rh, dims))


def partial_kernel(place_ref, coeff_ref, scale_ref, out_ref):
    per_half, big = out_ref.shape[1], out_ref.shape[2]
    coeff = coeff_ref[...]
    weighted = (coeff.astype(jnp.float32) * scale_ref[...]).astype(jnp.bfloat16)

    def add(first):
        for t, (i, j) in enumerate(packed(coeff.shape[0] // big)):
            part = mul(weighted[big * i : big * i + big], coeff[big * j : big * j + big], NT)
            spot = (t // per_half) ^ place_ref[2]
            if first:
                out_ref[spot, t % per_half] = part
            else:
                out_ref[spot, t % per_half] = out_ref[spot, t % per_half] + part

    @pl.when(pl.program_id(0) == 0)
    def _():
        add(True)

    @pl.when(pl.program_id(0) > 0)
    def _():
        add(False)


def packed(count):
    return [(i, j) for i in range(count) for j in range(i + 1)]


def partial_diag(place, coeff, scale):
    rows, cells = coeff.shape
    depth = min(DEPTH, cells)
    per_half = (rows // BIG) * (rows // BIG + 1) // 4
    shape = (2, per_half, BIG, BIG)
    return pl.pallas_call(
        partial_kernel,
        out_shape=jax.ShapeDtypeStruct(shape, jnp.float32),
        grid=(cells // depth,),
        in_specs=[
            SMEM,
            pl.BlockSpec((rows, depth), lambda k: (0, k)),
            pl.BlockSpec((1, depth), lambda k: (0, k)),
        ],
        out_specs=pl.BlockSpec(shape, lambda k: (0, 0, 0, 0)),
        compiler_params=params(),
        cost_estimate=pl.CostEstimate(
            flops=rows * rows * cells * 2, bytes_accessed=rows * cells * 2, transcendentals=0
        ),
        name="partial_diag",
    )(place, coeff, scale)


def triple_sum(rows):
    rows = rows.astype(jnp.float32)
    return rows[0:1] + rows[1:2] + rows[2:3]


def shared_kernel(place_ref, partners_ref, coeff_ref, own_ref, held_ref, partial_ref, out_ref):
    per_half, big = out_ref.shape[1], out_ref.shape[2]
    blocks, rounds = held_ref.shape[0], held_ref.shape[2] // SLOT
    block, core = place_ref[0], place_ref[2]
    scales = []
    for turn in range(rounds):
        cells = slice(SLOT * turn, SLOT * turn + SLOT)
        listed = partners_ref[turn, block]
        mate = jnp.int32(0)
        for other in range(blocks):
            mate = jnp.where(partners_ref[turn, other] == block, other, mate)
        theirs = triple_sum(held_ref[mate, held_ref.shape[1] - TRIPLE :, cells])
        scales.append(jnp.where(listed >= 0, own_ref[:, cells], theirs))
    scale = jnp.concatenate(scales, axis=1)
    coeff = coeff_ref[...]
    weighted = (coeff.astype(jnp.float32) * scale).astype(jnp.bfloat16)
    for t, (i, j) in enumerate(packed(coeff.shape[0] // big)):
        part = mul(weighted[big * i : big * i + big], coeff[big * j : big * j + big], NT)
        spot = (t // per_half) ^ core
        out_ref[spot, t % per_half] = partial_ref[spot, t % per_half] + part


def add_shared(place, partners, coeff, own_var, held, partial):
    return pl.pallas_call(
        shared_kernel,
        out_shape=jax.ShapeDtypeStruct(partial.shape, jnp.float32),
        in_specs=[SMEM, SMEM, VMEM, VMEM, VMEM, VMEM],
        out_specs=VMEM,
        input_output_aliases={5: 0},
        compiler_params=params(),
        name="add_shared",
    )(place, partners, coeff, own_var, held, partial)


def pack_kernel(place_ref, coeff_ref, var_ref, pieces_ref, *rows_refs):
    chunk = pieces_ref.shape[1] - TRIPLE
    quarter = rows_refs[0].shape[0] - TRIPLE
    var = var_ref[...]
    high = var.astype(jnp.bfloat16).astype(jnp.float32)
    middle = (var - high).astype(jnp.bfloat16).astype(jnp.float32)
    low = var - high - middle
    line = lax.broadcasted_iota(jnp.int32, (TRIPLE, var.shape[1]), 0)
    triple = jnp.where(line == 0, high, jnp.where(line == 1, middle, jnp.where(line == 2, low, 0.0)))
    triple = triple.astype(jnp.bfloat16)
    for block in range(pieces_ref.shape[0]):
        pieces_ref[block, :chunk] = coeff_ref[chunk * block : chunk * block + chunk]
        pieces_ref[block, chunk:] = triple
    for step, rows_ref in enumerate(rows_refs):
        start = pl.multiple_of((place_ref[1] ^ step) * quarter, quarter)
        rows_ref[:quarter] = coeff_ref[pl.ds(start, quarter)]
        rows_ref[quarter:] = triple


def pack(place, coeff, var, blocks, slabs):
    rows, cells = coeff.shape
    return pl.pallas_call(
        pack_kernel,
        out_shape=[jax.ShapeDtypeStruct((blocks, rows // blocks + TRIPLE, cells), coeff.dtype)]
        + [jax.ShapeDtypeStruct((rows // slabs + TRIPLE, cells), coeff.dtype)] * slabs,
        in_specs=[SMEM, VMEM, VMEM],
        out_specs=[VMEM] * (slabs + 1),
        compiler_params=params(),
        name="pack",
    )(place, coeff, var)


def row_bcast(x, j):
    return jnp.broadcast_to(x[j:j+1, :], (SUB, NB))

def col_bcast(x, c):
    return jnp.broadcast_to(x[:, c:c+1], (SUB, NB))

def factor_columns(columns, inverse):
    out = []
    for k in range(SUB):
        column = columns[0] * row_bcast(inverse[0], k)
        for j in range(1, k+1):
            column = column + columns[j] * row_bcast(inverse[j], k)
        out.append(column)
    return out

def factor_tile(tile):
    groups = NB // SUB
    sub = lax.broadcasted_iota(jnp.int32, (SUB, NB), 0)
    lane = lax.broadcasted_iota(jnp.int32, (SUB, NB), 1)
    W = [tile[SUB*g:SUB*g+SUB, :] for g in range(groups)]
    V = [(lane == sub + SUB*g).astype(jnp.float32) for g in range(groups)]
    ups, invs = [], []
    dcol = [col_bcast(W[0], j) for j in range(SUB)]
    left = [col_bcast(W[1], j) for j in range(SUB)]
    right = [col_bcast(W[1], SUB+j) for j in range(SUB)]
    for g in range(groups):
        icol = [(sub == j).astype(jnp.float32) for j in range(SUB)]
        for k in range(SUB):
            r = lax.rsqrt(row_bcast(dcol[k], k))
            lk = dcol[k] * r
            r2 = r * r
            for j in range(k+1, SUB):
                dcol[j] = dcol[j] - (dcol[k] * row_bcast(dcol[k], j)) * r2
            below = jnp.where(sub > k, lk, 0.0)
            for j in range(k+1):
                a = row_bcast(icol[j], k) * r
                icol[j] = jnp.where(sub == k, a, icol[j] - below * a)
        R, S = W[g], V[g]
        U = icol[0] * row_bcast(R, 0)
        SV = icol[0] * row_bcast(S, 0)
        for j in range(1, SUB):
            U = U + icol[j] * row_bcast(R, j)
            SV = SV + icol[j] * row_bcast(S, j)
        U = jnp.where(lane >= sub + SUB*g, U, 0.0)
        ups.append(U); invs.append(SV)
        if g + 1 == groups:
            break
        first = factor_columns(left, icol)
        dcol = right
        for k in range(SUB):
            for j in range(SUB):
                dcol[j] = dcol[j] - first[k] * row_bcast(first[k], j)
            W[g+1] = W[g+1] - first[k] * row_bcast(U, k)
            V[g+1] = V[g+1] - first[k] * row_bcast(SV, k)
        if g + 2 == groups:
            continue
        second = factor_columns([col_bcast(W[g+2], SUB*g+j) for j in range(SUB)], icol)
        left = [col_bcast(W[g+2], SUB*(g+1)+j) for j in range(SUB)]
        right = [col_bcast(W[g+2], SUB*(g+2)+j) for j in range(SUB)]
        for k in range(SUB):
            for j in range(SUB):
                left[j] = left[j] - second[k] * row_bcast(first[k], j)
                right[j] = right[j] - second[k] * row_bcast(second[k], j)
            W[g+2] = W[g+2] - second[k] * row_bcast(U, k)
            V[g+2] = V[g+2] - second[k] * row_bcast(SV, k)
        if g + 3 < groups:
            uh = U.astype(jnp.bfloat16).astype(jnp.float32)
            ul = U - uh
            sh = SV.astype(jnp.bfloat16).astype(jnp.float32)
            sl = SV - sh
            zero = jnp.zeros((SUB, NB), jnp.float32)
            lhs = jnp.concatenate([uh, ul, uh, zero], 0).astype(jnp.bfloat16)
            rhs = jnp.concatenate([
                jnp.concatenate([uh, uh, ul, zero], 0),
                jnp.concatenate([sh, sh, sl, zero], 0)], 1).astype(jnp.bfloat16)
            upd = lax.dot_general(lhs, rhs, (((0,), (0,)), ((), ())), preferred_element_type=jnp.float32)
            for t in range(g+3, groups):
                W[t] = W[t] - upd[SUB*t:SUB*t+SUB, :NB]
                V[t] = V[t] - upd[SUB*t:SUB*t+SUB, NB:]
    return jnp.concatenate(ups, 0), jnp.concatenate(invs, 0)


def chol_kernel(place_ref, mine_ref, other_ref, ct_ref, lrow_ref, zt_ref, M):
    n = zt_ref.shape[1]
    cb = n // NB
    extra = ct_ref.shape[0]
    total = n + extra
    quarter = lrow_ref.shape[0]
    big = mine_ref.shape[1]
    nbig = n // big
    half = mine_ref.shape[0]
    per = big // NB
    is0 = place_ref[2] == 0
    for i in range(nbig):
        for j in range(i+1):
            t = tri(i, j)
            if t < half:
                x = jnp.where(is0, mine_ref[t], other_ref[t])
            else:
                x = jnp.where(is0, other_ref[t-half], mine_ref[t-half])
            for b in range(per):
                M[j*per+b, big*i:big*i+big, :] = x[:, NB*b:NB*b+NB]
    for q in range(cb):
        M[q, n:total, :] = ct_ref[:, NB*q:NB*q+NB]

    def step_rest(p, inv):
        inv_parts = halves(inv)
        lo = (p+1)*NB
        below = mul3(halves(M[p, lo:total, :]), inv_parts)
        M[p, lo:total, :] = below
        high, low = halves(below)
        q = p + 1
        while q < cb:
            w = 2 if q + 1 < cb else 1
            a = (q - p - 1)*NB
            acc = mul3((high[a:], low[a:]), (high[a:a+w*NB], low[a:a+w*NB]))
            for b in range(w):
                M[q+b, q*NB:total, :] = M[q+b, q*NB:total, :] - acc[:, b*NB:b*NB+NB]
            q += w

    def body(p, carry):
        rows = pl.ds(pl.multiple_of(p*NB, NB), NB)
        up, inv = factor_tile(M[p, rows, :])
        M[p, rows, :] = up.T
        for s in range(cb):
            @pl.when(p == s)
            def _():
                step_rest(s, inv)
        return carry
    lax.fori_loop(0, cb, body, 0)
    start = pl.multiple_of(place_ref[1]*quarter, quarter)
    ids = lax.broadcasted_iota(jnp.int32, (quarter, NB), 0) + start
    for q in range(cb):
        lrow_ref[:, NB*q:NB*q+NB] = jnp.where(ids >= q*NB, M[q, pl.ds(start, quarter), :], 0.0)
        zt_ref[:, NB*q:NB*q+NB] = M[q, n:total, :]

def chol_solve(place, mine, other, ct, quarter):
    n = ct.shape[1]
    extra = ct.shape[0]
    return pl.pallas_call(
        chol_kernel,
        out_shape=(jax.ShapeDtypeStruct((quarter, n), jnp.float32), jax.ShapeDtypeStruct((extra, n), jnp.float32)),
        in_specs=[SMEM, VMEM, VMEM, VMEM],
        out_specs=(VMEM, VMEM),
        scratch_shapes=[pltpu.VMEM((n//NB, n+extra, NB), jnp.float32)],
        compiler_params=params(),
        cost_estimate=pl.CostEstimate(flops=40 * 10**9, bytes_accessed=8 * n * n, transcendentals=0),
        name="factor_solve",
    )(place, mine, other, ct)


def unpack_kernel(place_ref, mine_ref, other_ref, out_ref):
    per_half, big = mine_ref.shape[0], mine_ref.shape[1]
    row = place_ref[1]
    for t in range(out_ref.shape[1] // big):
        high, low = jnp.maximum(row, t), jnp.minimum(row, t)
        spot = high * (high + 1) // 2 + low
        upper = (spot >= per_half).astype(jnp.int32)
        slot = spot - upper * per_half
        tile = jnp.where(upper == place_ref[2], mine_ref[slot], other_ref[slot])
        out_ref[:, big * t : big * t + big] = jnp.where(row < t, tile.T, tile)


def unpack_rows(place, mine, other, rows):
    return pl.pallas_call(
        unpack_kernel,
        out_shape=jax.ShapeDtypeStruct((mine.shape[1], rows), jnp.float32),
        in_specs=[SMEM, VMEM, VMEM],
        out_specs=VMEM,
        compiler_params=params(),
        name="diag_rows",
    )(place, mine, other)


def forward_kernel(partners_ref, held_ref, out_ref):
    blocks, chunk, cells = out_ref.shape
    rounds = cells // SLOT
    for block in range(blocks):
        for turn in range(rounds):
            source = jnp.maximum(partners_ref[turn, block], 0)
            columns = slice(SLOT * turn, SLOT * turn + SLOT)
            out_ref[block, :, columns] = held_ref[source, :chunk, columns]


def forward(partners, held):
    return pl.pallas_call(
        forward_kernel,
        out_shape=jax.ShapeDtypeStruct((held.shape[0], held.shape[1] - TRIPLE, held.shape[2]), held.dtype),
        in_specs=[SMEM, VMEM],
        out_specs=VMEM,
        compiler_params=params(),
        name="forward",
    )(partners, held)


def row_weights(row_refs, cells):
    pieces = []
    for ref in row_refs:
        quarter = ref.shape[0] - TRIPLE
        pieces.append(ref[:quarter, cells].astype(jnp.float32) * triple_sum(ref[quarter:, cells]))
    return halves(jnp.concatenate(pieces, axis=1))


def tiles_kernel(place_ref, partners_ref, *refs):
    row_refs, other_refs, out_ref = refs[:4], refs[4:8], refs[8]
    rows, rounds = other_refs[0].shape[0], other_refs[0].shape[1] // SLOT
    for turn in range(rounds):
        cells = slice(SLOT * turn, SLOT * turn + SLOT)
        high, low = row_weights(row_refs, cells)
        other = jnp.concatenate([x[:, cells] for x in other_refs], axis=1)
        tile = mul(high, other, NT) + mul(low, other, NT)
        listed = partners_ref[turn, place_ref[0]] >= 0
        out_ref[:, rows * turn : rows * turn + rows] = jnp.where(listed, tile, 0.0)


def pair_tiles(place, partners, own_rows, others):
    quarter, (rows, cells) = own_rows[0].shape[0] - TRIPLE, others[0].shape
    return pl.pallas_call(
        tiles_kernel,
        out_shape=jax.ShapeDtypeStruct((quarter, cells // SLOT * rows), jnp.float32),
        in_specs=[SMEM, SMEM] + [VMEM] * 8,
        out_specs=VMEM,
        compiler_params=params(),
        cost_estimate=pl.CostEstimate(flops=3 * 10**9, bytes_accessed=5 * 10**6, transcendentals=0),
        name="pair_tiles",
    )(place, partners, *own_rows, *others)


def solved_sum(place_ref, partners_ref, row_refs, high_refs, low_refs):
    rounds = row_refs[0].shape[1] // SLOT
    first, second = 0.0, 0.0
    for turn in range(rounds):
        cells = slice(SLOT * turn, SLOT * turn + SLOT)
        high = jnp.concatenate([x[cells, :] for x in high_refs], axis=0)
        low = jnp.concatenate([x[cells, :] for x in low_refs], axis=0)
        solved = mul3(row_weights(row_refs, cells), (high, low), NN)
        listed = partners_ref[turn, place_ref[0]]
        first = first + jnp.where(listed == 0, solved, 0.0)
        second = second + jnp.where(listed == 1, solved, 0.0)
    return first, second


def near_kernel(place_ref, partners_ref, *refs):
    factor_ref, zero_ref, one_ref = refs[6:]
    first, second = solved_sum(place_ref, partners_ref, refs[:2], refs[2:4], refs[4:6])
    zero_ref[...] = jnp.where(place_ref[0] == 0, factor_ref[...], first)
    one_ref[...] = jnp.where(place_ref[0] == 1, factor_ref[...], second)


def far_kernel(place_ref, partners_ref, *refs):
    near_zero_ref, near_one_ref, zero_ref, one_ref = refs[6:]
    first, second = solved_sum(place_ref, partners_ref, refs[:2], refs[2:4], refs[4:6])
    zero_ref[...] = near_zero_ref[...] + jnp.where(place_ref[0] == 0, 0.0, first)
    one_ref[...] = near_one_ref[...] + jnp.where(place_ref[0] == 1, 0.0, second)


def chosen_sum(place_ref, partners_ref, row_refs, high_refs, low_refs):
    block = place_ref[0]
    later = partners_ref[1, block]
    is_later = jnp.logical_or(later == 0, later == 1)
    listed = jnp.where(is_later, later, partners_ref[0, block])
    pieces = []
    for ref in row_refs:
        quarter = ref.shape[0] - TRIPLE
        parts = []
        for turn in range(2):
            cells = slice(SLOT * turn, SLOT * turn + SLOT)
            parts.append(ref[:quarter, cells].astype(jnp.float32) * triple_sum(ref[quarter:, cells]))
        pieces.append(jnp.where(is_later, parts[1], parts[0]))
    weight = halves(jnp.concatenate(pieces, axis=1))
    high = jnp.concatenate([x[...] for x in high_refs], axis=0)
    low = jnp.concatenate([x[...] for x in low_refs], axis=0)
    solved = mul3(weight, (high, low), NN)
    return jnp.where(listed == 0, solved, 0.0), jnp.where(listed == 1, solved, 0.0)


def near_chosen_kernel(place_ref, partners_ref, *refs):
    factor_ref, zero_ref, one_ref = refs[6:]
    first, second = chosen_sum(place_ref, partners_ref, refs[:2], refs[2:4], refs[4:6])
    zero_ref[...] = jnp.where(place_ref[0] == 0, factor_ref[...], first)
    one_ref[...] = jnp.where(place_ref[0] == 1, factor_ref[...], second)


def far_chosen_kernel(place_ref, partners_ref, *refs):
    near_zero_ref, near_one_ref, zero_ref, one_ref = refs[6:]
    first, second = chosen_sum(place_ref, partners_ref, refs[:2], refs[2:4], refs[4:6])
    zero_ref[...] = near_zero_ref[...] + jnp.where(place_ref[0] == 0, 0.0, first)
    one_ref[...] = near_one_ref[...] + jnp.where(place_ref[0] == 1, 0.0, second)


def panels(kernel, place, partners, own_rows, highs, lows, more):
    shape = jax.ShapeDtypeStruct((own_rows[0].shape[0] - TRIPLE, highs[0].shape[1]), jnp.float32)
    return pl.pallas_call(
        kernel,
        out_shape=(shape, shape),
        in_specs=[SMEM, SMEM] + [VMEM] * (6 + len(more)),
        out_specs=(VMEM, VMEM),
        compiler_params=params(),
        cost_estimate=pl.CostEstimate(flops=3 * 10**9, bytes_accessed=5 * 10**6, transcendentals=0),
        name=kernel.__name__[:-7] + "_panels",
    )(place, partners, *own_rows, *highs, *lows, *more)


def spread(array, axis, root):
    mine = lax.axis_index(axis) == root
    return lax.psum(jnp.where(mine, array, jnp.zeros_like(array)), axis)


def exact_nt(left, right):
    return lax.dot_general(
        left, right, NT, precision=lax.Precision.HIGHEST, preferred_element_type=jnp.float32
    )


def coupled_panel(panel0, diag_part, tile_part, own_row, block_id, slab_id):
    quarter = panel0.shape[0]
    left_part, second_part = spread(panel0, "blk", 1), spread(diag_part, "blk", 1)
    left_full = lax.all_gather(left_part, "slab", axis=0, tiled=True)
    second_full = lax.all_gather(second_part, "slab", axis=0, tiled=True)
    second_factor = jnp.linalg.cholesky(second_full - exact_nt(left_full, left_full))
    col_second = jnp.sum(jnp.where((own_row == 1)[None, :, None], tile_part, 0.0), axis=1)
    rest = col_second - exact_nt(panel0, left_full)
    solved = jax.scipy.linalg.solve_triangular(second_factor, rest.T, lower=True).T
    second_rows = lax.dynamic_slice_in_dim(second_factor, slab_id * quarter, quarter, 0)
    return jnp.where(
        block_id == 0, jnp.zeros_like(solved), jnp.where(block_id == 1, second_rows, solved)
    )


def swap(array, step):
    return lax.ppermute(array, "slab", [(i, i ^ step) for i in range(lax.axis_size("slab"))])


def unscaled_halves(array):
    array = array.astype(jnp.float32) * (1.0 / SOLVE_SCALE)
    high = lax.reduce_precision(array, 8, 7)
    return high.astype(jnp.bfloat16), (array - high).astype(jnp.bfloat16)


def on_device(priv_coeff, priv_var, shared_coeff, shared_var, partners):
    rows = priv_coeff.shape[0]
    blocks, rounds = partners.shape
    block_id = lax.axis_index("blk").astype(jnp.int32)
    slab_id = lax.axis_index("slab").astype(jnp.int32)
    slabs = lax.axis_size("slab")
    quarter = rows // slabs
    place = jnp.stack([block_id, slab_id, slab_id % 2])
    table = partners.T

    pieces, *own_rows = pack(place, shared_coeff, shared_var, blocks, slabs)
    held = lax.all_to_all(pieces, "blk", 0, 0, tiled=True)
    own_rows = [swap(x, step) if step else x for step, x in enumerate(own_rows)]

    partial = partial_diag(place, priv_coeff, priv_var)
    partial, held, own_rows = lax.optimization_barrier((partial, held, own_rows))
    partial = add_shared(place, table, shared_coeff, shared_var, held, partial)
    up, down = DIAG_SCALE, 1.0 / DIAG_SCALE
    near = partial[0] + swap((partial[1] * up).astype(jnp.float16), 1).astype(jnp.float32) * down
    leaving, held = lax.optimization_barrier(((near * up).astype(jnp.float16), held))
    across = swap(leaving, 2)

    mate_coeff = lax.all_to_all(forward(table, held), "blk", 0, 0, tiled=True).reshape(rows, -1)
    across, mate_coeff = lax.optimization_barrier((across, mate_coeff))
    mine = near + across.astype(jnp.float32) * down

    from_zero, from_one = partners == 0, partners == 1
    one_each = jnp.logical_not(jnp.any(jnp.any(from_zero, axis=1) & jnp.any(from_one, axis=1)))
    is_coupled = jnp.any(from_zero[1])
    is_simple = one_each & jnp.logical_not(is_coupled)
    later = from_zero[:, 1] | from_one[:, 1]
    zero_later = jnp.where(later, from_zero[:, 1], from_zero[:, 0])
    choice = jnp.where(zero_later, 0, 2) + later.astype(jnp.int32)
    mine, choice, is_simple, is_coupled = lax.optimization_barrier((mine, choice, is_simple, is_coupled))

    other = swap(mine, 1)
    others = [swap(mate_coeff, step) if step else mate_coeff for step in (0, 1, 2)]
    cells = SLOT // blocks
    turned = shared_coeff.reshape(rows, rounds, blocks, cells).transpose(2, 1, 3, 0)
    turned = turned.reshape(rounds * SLOT, rows).astype(jnp.float32)
    factor_rows, solved = chol_solve(place, mine, other, turned, quarter)
    out = (solved * SOLVE_SCALE).astype(jnp.float16).reshape(blocks, rounds * cells, rows)
    spread_out = lax.all_to_all(out, "blk", 0, 0, tiled=True)
    diag_part = unpack_rows(place, mine, other, rows)
    _, others = lax.optimization_barrier((out, others))
    others = others + [swap(others[2], 1)]
    spread_out, diag_part = lax.optimization_barrier((spread_out, diag_part))

    sources = [spread_out[i, cells * turn : cells * turn + cells] for i in (0, 1) for turn in (0, 1)]
    onward = jnp.broadcast_to(sources[0][None], (blocks, cells, rows))
    for number, source in enumerate(sources[1:], 1):
        onward = jnp.where((choice == number)[:, None, None], source[None], onward)
    arrived = lax.all_to_all(onward, "blk", 0, 0, tiled=True)
    tile_part = pair_tiles(place, table, own_rows, others).reshape(quarter, rounds, rows)
    arrived, tile_part = lax.optimization_barrier((arrived, tile_part))

    def near_half(arrived, kernel):
        beside, across = swap(arrived, 1), swap(arrived, 2)
        highs, lows = zip(*[unscaled_halves(x) for x in (arrived, beside)])
        close = panels(kernel, place, table, own_rows[:2], highs, lows, (factor_rows,))
        across, close = lax.optimization_barrier((across, close))
        highs, lows = zip(*[unscaled_halves(x) for x in (across, swap(across, 1))])
        return highs, lows, close

    highs, lows, close = near_half(arrived.reshape(SLOT, rows), near_chosen_kernel)

    def simple():
        return panels(far_chosen_kernel, place, table, own_rows[2:], highs, lows, close)

    def general():
        wanted = jnp.repeat(from_zero, cells, axis=1)[:, :, None]
        both = jnp.where(wanted, spread_out[0][None], spread_out[1][None])
        both = lax.all_to_all(both, "blk", 0, 0, tiled=True).reshape(blocks, rounds, cells, rows)
        both = both.transpose(1, 0, 2, 3).reshape(solved.shape)
        highs, lows, close = near_half(both, near_kernel)
        panel0, panel1 = panels(far_kernel, place, table, own_rows[2:], highs, lows, close)
        own_row = lax.dynamic_index_in_dim(partners, block_id, 0, False)
        panel1 = lax.cond(
            is_coupled,
            lambda: coupled_panel(panel0, diag_part, tile_part, own_row, block_id, slab_id),
            lambda: panel1,
        )
        return panel0, panel1

    panel0, panel1 = lax.cond(is_simple, simple, general)
    return (diag_part[None], tile_part[None], panel0, panel1)


def solution(mesh):
    in_specs = (P("blk", "slab"), P("blk", "slab"), P("blk", "slab"), P("blk", "slab"), P())
    out_specs = (
        P("blk", "slab", None),
        P("blk", "slab", None, None),
        P(("blk", "slab"), None),
        P(("blk", "slab"), None),
    )
    return jax.shard_map(
        on_device, mesh=mesh, in_specs=in_specs, out_specs=out_specs, check_vma=False
    )
```

```python
import functools

import jax
import jax.numpy as jnp
from jax import lax
from jax.experimental import pallas as pl
from jax.experimental.pallas import tpu as pltpu
from jax.sharding import PartitionSpec as P

SLOT = 128
NB = 128
SUB = 8
BIG = 256
TRIPLE = 16
DEPTH = 1024
DIAG_SCALE = 256.0
SOLVE_SCALE = 4096.0
SMEM = pl.BlockSpec(memory_space=pltpu.SMEM)
VMEM = pl.BlockSpec(memory_space=pltpu.VMEM)
NT = (((1,), (1,)), ((), ()))
NN = (((1,), (0,)), ((), ()))


def params():
    return pltpu.CompilerParams(vmem_limit_bytes=48 * 1024 * 1024)


def tri(i, j):
    return i * (i + 1) // 2 + j


def halves(x):
    hi = x.astype(jnp.bfloat16)
    return hi, (x - hi.astype(jnp.float32)).astype(jnp.bfloat16)


def mul(left, right, dims):
    return lax.dot_general(left, right, dims, preferred_element_type=jnp.float32)


def mul3(left, right, dims=NT):
    (lh, ll), (rh, rl) = left, right
    return mul(lh, rh, dims) + (mul(lh, rl, dims) + mul(ll, rh, dims))


def partial_kernel(place_ref, coeff_ref, scale_ref, out_ref):
    per_half, big = out_ref.shape[1], out_ref.shape[2]
    coeff = coeff_ref[...]
    weighted = (coeff.astype(jnp.float32) * scale_ref[...]).astype(jnp.bfloat16)

    def add(first):
        for t, (i, j) in enumerate(packed(coeff.shape[0] // big)):
            part = mul(weighted[big * i : big * i + big], coeff[big * j : big * j + big], NT)
            spot = (t // per_half) ^ place_ref[2]
            if first:
                out_ref[spot, t % per_half] = part
            else:
                out_ref[spot, t % per_half] = out_ref[spot, t % per_half] + part

    @pl.when(pl.program_id(0) == 0)
    def _():
        add(True)

    @pl.when(pl.program_id(0) > 0)
    def _():
        add(False)


def packed(count):
    return [(i, j) for i in range(count) for j in range(i + 1)]


def partial_diag(place, coeff, scale):
    rows, cells = coeff.shape
    depth = min(DEPTH, cells)
    per_half = (rows // BIG) * (rows // BIG + 1) // 4
    shape = (2, per_half, BIG, BIG)
    return pl.pallas_call(
        partial_kernel,
        out_shape=jax.ShapeDtypeStruct(shape, jnp.float32),
        grid=(cells // depth,),
        in_specs=[
            SMEM,
            pl.BlockSpec((rows, depth), lambda k: (0, k)),
            pl.BlockSpec((1, depth), lambda k: (0, k)),
        ],
        out_specs=pl.BlockSpec(shape, lambda k: (0, 0, 0, 0)),
        compiler_params=params(),
        cost_estimate=pl.CostEstimate(
            flops=rows * rows * cells * 2, bytes_accessed=rows * cells * 2, transcendentals=0
        ),
        name="partial_diag",
    )(place, coeff, scale)


def triple_sum(rows):
    rows = rows.astype(jnp.float32)
    return rows[0:1] + rows[1:2] + rows[2:3]


def shared_kernel(place_ref, partners_ref, coeff_ref, own_ref, held_ref, partial_ref, out_ref):
    per_half, big = out_ref.shape[1], out_ref.shape[2]
    blocks, rounds = held_ref.shape[0], held_ref.shape[2] // SLOT
    block, core = place_ref[0], place_ref[2]
    scales = []
    for turn in range(rounds):
        cells = slice(SLOT * turn, SLOT * turn + SLOT)
        listed = partners_ref[turn, block]
        mate = jnp.int32(0)
        for other in range(blocks):
            mate = jnp.where(partners_ref[turn, other] == block, other, mate)
        theirs = triple_sum(held_ref[mate, held_ref.shape[1] - TRIPLE :, cells])
        scales.append(jnp.where(listed >= 0, own_ref[:, cells], theirs))
    scale = jnp.concatenate(scales, axis=1)
    coeff = coeff_ref[...]
    weighted = (coeff.astype(jnp.float32) * scale).astype(jnp.bfloat16)
    for t, (i, j) in enumerate(packed(coeff.shape[0] // big)):
        part = mul(weighted[big * i : big * i + big], coeff[big * j : big * j + big], NT)
        spot = (t // per_half) ^ core
        out_ref[spot, t % per_half] = partial_ref[spot, t % per_half] + part


def add_shared(place, partners, coeff, own_var, held, partial):
    return pl.pallas_call(
        shared_kernel,
        out_shape=jax.ShapeDtypeStruct(partial.shape, jnp.float32),
        in_specs=[SMEM, SMEM, VMEM, VMEM, VMEM, VMEM],
        out_specs=VMEM,
        input_output_aliases={5: 0},
        compiler_params=params(),
        name="add_shared",
    )(place, partners, coeff, own_var, held, partial)


def pack_kernel(place_ref, coeff_ref, var_ref, pieces_ref, *rows_refs):
    chunk = pieces_ref.shape[1] - TRIPLE
    quarter = rows_refs[0].shape[0] - TRIPLE
    var = var_ref[...]
    high = var.astype(jnp.bfloat16).astype(jnp.float32)
    middle = (var - high).astype(jnp.bfloat16).astype(jnp.float32)
    low = var - high - middle
    line = lax.broadcasted_iota(jnp.int32, (TRIPLE, var.shape[1]), 0)
    triple = jnp.where(line == 0, high, jnp.where(line == 1, middle, jnp.where(line == 2, low, 0.0)))
    triple = triple.astype(jnp.bfloat16)
    for block in range(pieces_ref.shape[0]):
        pieces_ref[block, :chunk] = coeff_ref[chunk * block : chunk * block + chunk]
        pieces_ref[block, chunk:] = triple
    for step, rows_ref in enumerate(rows_refs):
        start = pl.multiple_of((place_ref[1] ^ step) * quarter, quarter)
        rows_ref[:quarter] = coeff_ref[pl.ds(start, quarter)]
        rows_ref[quarter:] = triple


def pack(place, coeff, var, blocks, slabs):
    rows, cells = coeff.shape
    return pl.pallas_call(
        pack_kernel,
        out_shape=[jax.ShapeDtypeStruct((blocks, rows // blocks + TRIPLE, cells), coeff.dtype)]
        + [jax.ShapeDtypeStruct((rows // slabs + TRIPLE, cells), coeff.dtype)] * slabs,
        in_specs=[SMEM, VMEM, VMEM],
        out_specs=[VMEM] * (slabs + 1),
        compiler_params=params(),
        name="pack",
    )(place, coeff, var)


def row_bcast(x, j):
    return jnp.broadcast_to(x[j:j+1, :], (SUB, NB))

def col_bcast(x, c):
    return jnp.broadcast_to(x[:, c:c+1], (SUB, NB))

def factor_columns(columns, inverse):
    out = []
    for k in range(SUB):
        column = columns[0] * row_bcast(inverse[0], k)
        for j in range(1, k+1):
            column = column + columns[j] * row_bcast(inverse[j], k)
        out.append(column)
    return out

def factor_tile(tile):
    groups = NB // SUB
    sub = lax.broadcasted_iota(jnp.int32, (SUB, NB), 0)
    lane = lax.broadcasted_iota(jnp.int32, (SUB, NB), 1)
    W = [tile[SUB*g:SUB*g+SUB, :] for g in range(groups)]
    V = [(lane == sub + SUB*g).astype(jnp.float32) for g in range(groups)]
    ups, invs = [], []
    dcol = [col_bcast(W[0], j) for j in range(SUB)]
    left = [col_bcast(W[1], j) for j in range(SUB)]
    right = [col_bcast(W[1], SUB+j) for j in range(SUB)]
    for g in range(groups):
        icol = [(sub == j).astype(jnp.float32) for j in range(SUB)]
        for k in range(SUB):
            r = lax.rsqrt(row_bcast(dcol[k], k))
            lk = dcol[k] * r
            r2 = r * r
            for j in range(k+1, SUB):
                dcol[j] = dcol[j] - (dcol[k] * row_bcast(dcol[k], j)) * r2
            below = jnp.where(sub > k, lk, 0.0)
            for j in range(k+1):
                a = row_bcast(icol[j], k) * r
                icol[j] = jnp.where(sub == k, a, icol[j] - below * a)
        R, S = W[g], V[g]
        U = icol[0] * row_bcast(R, 0)
        SV = icol[0] * row_bcast(S, 0)
        for j in range(1, SUB):
            U = U + icol[j] * row_bcast(R, j)
            SV = SV + icol[j] * row_bcast(S, j)
        U = jnp.where(lane >= sub + SUB*g, U, 0.0)
        ups.append(U); invs.append(SV)
        if g + 1 == groups:
            break
        first = factor_columns(left, icol)
        dcol = right
        for k in range(SUB):
            for j in range(SUB):
                dcol[j] = dcol[j] - first[k] * row_bcast(first[k], j)
            W[g+1] = W[g+1] - first[k] * row_bcast(U, k)
            V[g+1] = V[g+1] - first[k] * row_bcast(SV, k)
        if g + 2 == groups:
            continue
        second = factor_columns([col_bcast(W[g+2], SUB*g+j) for j in range(SUB)], icol)
        left = [col_bcast(W[g+2], SUB*(g+1)+j) for j in range(SUB)]
        right = [col_bcast(W[g+2], SUB*(g+2)+j) for j in range(SUB)]
        for k in range(SUB):
            for j in range(SUB):
                left[j] = left[j] - second[k] * row_bcast(first[k], j)
                right[j] = right[j] - second[k] * row_bcast(second[k], j)
            W[g+2] = W[g+2] - second[k] * row_bcast(U, k)
            V[g+2] = V[g+2] - second[k] * row_bcast(SV, k)
        if g + 3 < groups:
            uh = U.astype(jnp.bfloat16).astype(jnp.float32)
            ul = U - uh
            sh = SV.astype(jnp.bfloat16).astype(jnp.float32)
            sl = SV - sh
            zero = jnp.zeros((SUB, NB), jnp.float32)
            lhs = jnp.concatenate([uh, ul, uh, zero], 0).astype(jnp.bfloat16)
            rhs = jnp.concatenate([
                jnp.concatenate([uh, uh, ul, zero], 0),
                jnp.concatenate([sh, sh, sl, zero], 0)], 1).astype(jnp.bfloat16)
            upd = lax.dot_general(lhs, rhs, (((0,), (0,)), ((), ())), preferred_element_type=jnp.float32)
            for t in range(g+3, groups):
                W[t] = W[t] - upd[SUB*t:SUB*t+SUB, :NB]
                V[t] = V[t] - upd[SUB*t:SUB*t+SUB, NB:]
    return jnp.concatenate(ups, 0), jnp.concatenate(invs, 0)


def chol_kernel(place_ref, mine_ref, other_ref, ct_ref, lrow_ref, zt_ref, M):
    n = zt_ref.shape[1]
    cb = n // NB
    extra = ct_ref.shape[0]
    total = n + extra
    quarter = lrow_ref.shape[0]
    big = mine_ref.shape[1]
    nbig = n // big
    half = mine_ref.shape[0]
    per = big // NB
    is0 = place_ref[2] == 0
    for i in range(nbig):
        for j in range(i+1):
            t = tri(i, j)
            if t < half:
                x = jnp.where(is0, mine_ref[t], other_ref[t])
            else:
                x = jnp.where(is0, other_ref[t-half], mine_ref[t-half])
            for b in range(per):
                M[j*per+b, big*i:big*i+big, :] = x[:, NB*b:NB*b+NB]
    for q in range(cb):
        M[q, n:total, :] = ct_ref[:, NB*q:NB*q+NB]

    def step_rest(p, inv):
        inv_parts = halves(inv)
        lo = (p+1)*NB
        below = mul3(halves(M[p, lo:total, :]), inv_parts)
        M[p, lo:total, :] = below
        high, low = halves(below)
        q = p + 1
        while q < cb:
            w = 2 if q + 1 < cb else 1
            a = (q - p - 1)*NB
            acc = mul3((high[a:], low[a:]), (high[a:a+w*NB], low[a:a+w*NB]))
            for b in range(w):
                M[q+b, q*NB:total, :] = M[q+b, q*NB:total, :] - acc[:, b*NB:b*NB+NB]
            q += w

    def body(p, carry):
        rows = pl.ds(pl.multiple_of(p*NB, NB), NB)
        up, inv = factor_tile(M[p, rows, :])
        M[p, rows, :] = up.T
        for s in range(cb):
            @pl.when(p == s)
            def _():
                step_rest(s, inv)
        return carry
    lax.fori_loop(0, cb, body, 0)
    start = pl.multiple_of(place_ref[1]*quarter, quarter)
    ids = lax.broadcasted_iota(jnp.int32, (quarter, NB), 0) + start
    for q in range(cb):
        lrow_ref[:, NB*q:NB*q+NB] = jnp.where(ids >= q*NB, M[q, pl.ds(start, quarter), :], 0.0)
        zt_ref[:, NB*q:NB*q+NB] = M[q, n:total, :]

def chol_solve(place, mine, other, ct, quarter):
    n = ct.shape[1]
    extra = ct.shape[0]
    return pl.pallas_call(
        chol_kernel,
        out_shape=(jax.ShapeDtypeStruct((quarter, n), jnp.float32), jax.ShapeDtypeStruct((extra, n), jnp.float32)),
        in_specs=[SMEM, VMEM, VMEM, VMEM],
        out_specs=(VMEM, VMEM),
        scratch_shapes=[pltpu.VMEM((n//NB, n+extra, NB), jnp.float32)],
        compiler_params=params(),
        cost_estimate=pl.CostEstimate(flops=40 * 10**9, bytes_accessed=8 * n * n, transcendentals=0),
        name="factor_solve",
    )(place, mine, other, ct)


def unpack_kernel(place_ref, mine_ref, other_ref, out_ref):
    per_half, big = mine_ref.shape[0], mine_ref.shape[1]
    row = place_ref[1]
    for t in range(out_ref.shape[1] // big):
        high, low = jnp.maximum(row, t), jnp.minimum(row, t)
        spot = high * (high + 1) // 2 + low
        upper = (spot >= per_half).astype(jnp.int32)
        slot = spot - upper * per_half
        tile = jnp.where(upper == place_ref[2], mine_ref[slot], other_ref[slot])
        out_ref[:, big * t : big * t + big] = jnp.where(row < t, tile.T, tile)


def unpack_rows(place, mine, other, rows):
    return pl.pallas_call(
        unpack_kernel,
        out_shape=jax.ShapeDtypeStruct((mine.shape[1], rows), jnp.float32),
        in_specs=[SMEM, VMEM, VMEM],
        out_specs=VMEM,
        compiler_params=params(),
        name="diag_rows",
    )(place, mine, other)


def forward_kernel(partners_ref, held_ref, out_ref):
    blocks, chunk, cells = out_ref.shape
    rounds = cells // SLOT
    for block in range(blocks):
        for turn in range(rounds):
            source = jnp.maximum(partners_ref[turn, block], 0)
            columns = slice(SLOT * turn, SLOT * turn + SLOT)
            out_ref[block, :, columns] = held_ref[source, :chunk, columns]


def forward(partners, held):
    return pl.pallas_call(
        forward_kernel,
        out_shape=jax.ShapeDtypeStruct((held.shape[0], held.shape[1] - TRIPLE, held.shape[2]), held.dtype),
        in_specs=[SMEM, VMEM],
        out_specs=VMEM,
        compiler_params=params(),
        name="forward",
    )(partners, held)


def row_weights(row_refs, cells):
    pieces = []
    for ref in row_refs:
        quarter = ref.shape[0] - TRIPLE
        pieces.append(ref[:quarter, cells].astype(jnp.float32) * triple_sum(ref[quarter:, cells]))
    return halves(jnp.concatenate(pieces, axis=1))


def tiles_kernel(place_ref, partners_ref, *refs):
    row_refs, other_refs, out_ref = refs[:4], refs[4:8], refs[8]
    rows, rounds = other_refs[0].shape[0], other_refs[0].shape[1] // SLOT
    for turn in range(rounds):
        cells = slice(SLOT * turn, SLOT * turn + SLOT)
        high, low = row_weights(row_refs, cells)
        other = jnp.concatenate([x[:, cells] for x in other_refs], axis=1)
        tile = mul(high, other, NT) + mul(low, other, NT)
        listed = partners_ref[turn, place_ref[0]] >= 0
        out_ref[:, rows * turn : rows * turn + rows] = jnp.where(listed, tile, 0.0)


def pair_tiles(place, partners, own_rows, others):
    quarter, (rows, cells) = own_rows[0].shape[0] - TRIPLE, others[0].shape
    return pl.pallas_call(
        tiles_kernel,
        out_shape=jax.ShapeDtypeStruct((quarter, cells // SLOT * rows), jnp.float32),
        in_specs=[SMEM, SMEM] + [VMEM] * 8,
        out_specs=VMEM,
        compiler_params=params(),
        cost_estimate=pl.CostEstimate(flops=3 * 10**9, bytes_accessed=5 * 10**6, transcendentals=0),
        name="pair_tiles",
    )(place, partners, *own_rows, *others)


def solved_sum(place_ref, partners_ref, row_refs, high_refs, low_refs):
    rounds = row_refs[0].shape[1] // SLOT
    first, second = 0.0, 0.0
    for turn in range(rounds):
        cells = slice(SLOT * turn, SLOT * turn + SLOT)
        high = jnp.concatenate([x[cells, :] for x in high_refs], axis=0)
        low = jnp.concatenate([x[cells, :] for x in low_refs], axis=0)
        solved = mul3(row_weights(row_refs, cells), (high, low), NN)
        listed = partners_ref[turn, place_ref[0]]
        first = first + jnp.where(listed == 0, solved, 0.0)
        second = second + jnp.where(listed == 1, solved, 0.0)
    return first, second


def near_kernel(place_ref, partners_ref, *refs):
    factor_ref, zero_ref, one_ref = refs[6:]
    first, second = solved_sum(place_ref, partners_ref, refs[:2], refs[2:4], refs[4:6])
    zero_ref[...] = jnp.where(place_ref[0] == 0, factor_ref[...], first)
    one_ref[...] = jnp.where(place_ref[0] == 1, factor_ref[...], second)


def far_kernel(place_ref, partners_ref, *refs):
    near_zero_ref, near_one_ref, zero_ref, one_ref = refs[6:]
    first, second = solved_sum(place_ref, partners_ref, refs[:2], refs[2:4], refs[4:6])
    zero_ref[...] = near_zero_ref[...] + jnp.where(place_ref[0] == 0, 0.0, first)
    one_ref[...] = near_one_ref[...] + jnp.where(place_ref[0] == 1, 0.0, second)


def chosen_sum(place_ref, partners_ref, row_refs, high_refs, low_refs):
    block = place_ref[0]
    later = partners_ref[1, block]
    is_later = jnp.logical_or(later == 0, later == 1)
    listed = jnp.where(is_later, later, partners_ref[0, block])
    pieces = []
    for ref in row_refs:
        quarter = ref.shape[0] - TRIPLE
        parts = []
        for turn in range(2):
            cells = slice(SLOT * turn, SLOT * turn + SLOT)
            parts.append(ref[:quarter, cells].astype(jnp.float32) * triple_sum(ref[quarter:, cells]))
        pieces.append(jnp.where(is_later, parts[1], parts[0]))
    weight = halves(jnp.concatenate(pieces, axis=1))
    high = jnp.concatenate([x[...] for x in high_refs], axis=0)
    low = jnp.concatenate([x[...] for x in low_refs], axis=0)
    solved = mul3(weight, (high, low), NN)
    return jnp.where(listed == 0, solved, 0.0), jnp.where(listed == 1, solved, 0.0)


def near_chosen_kernel(place_ref, partners_ref, *refs):
    factor_ref, zero_ref, one_ref = refs[6:]
    first, second = chosen_sum(place_ref, partners_ref, refs[:2], refs[2:4], refs[4:6])
    zero_ref[...] = jnp.where(place_ref[0] == 0, factor_ref[...], first)
    one_ref[...] = jnp.where(place_ref[0] == 1, factor_ref[...], second)


def far_chosen_kernel(place_ref, partners_ref, *refs):
    near_zero_ref, near_one_ref, zero_ref, one_ref = refs[6:]
    first, second = chosen_sum(place_ref, partners_ref, refs[:2], refs[2:4], refs[4:6])
    zero_ref[...] = near_zero_ref[...] + jnp.where(place_ref[0] == 0, 0.0, first)
    one_ref[...] = near_one_ref[...] + jnp.where(place_ref[0] == 1, 0.0, second)


def panels(kernel, place, partners, own_rows, highs, lows, more):
    shape = jax.ShapeDtypeStruct((own_rows[0].shape[0] - TRIPLE, highs[0].shape[1]), jnp.float32)
    return pl.pallas_call(
        kernel,
        out_shape=(shape, shape),
        in_specs=[SMEM, SMEM] + [VMEM] * (6 + len(more)),
        out_specs=(VMEM, VMEM),
        compiler_params=params(),
        cost_estimate=pl.CostEstimate(flops=3 * 10**9, bytes_accessed=5 * 10**6, transcendentals=0),
        name=kernel.__name__[:-7] + "_panels",
    )(place, partners, *own_rows, *highs, *lows, *more)


def spread(array, axis, root):
    mine = lax.axis_index(axis) == root
    return lax.psum(jnp.where(mine, array, jnp.zeros_like(array)), axis)


def exact_nt(left, right):
    return lax.dot_general(
        left, right, NT, precision=lax.Precision.HIGHEST, preferred_element_type=jnp.float32
    )


def coupled_panel(panel0, diag_part, tile_part, own_row, block_id, slab_id):
    quarter = panel0.shape[0]
    left_part, second_part = spread(panel0, "blk", 1), spread(diag_part, "blk", 1)
    left_full = lax.all_gather(left_part, "slab", axis=0, tiled=True)
    second_full = lax.all_gather(second_part, "slab", axis=0, tiled=True)
    second_factor = jnp.linalg.cholesky(second_full - exact_nt(left_full, left_full))
    col_second = jnp.sum(jnp.where((own_row == 1)[None, :, None], tile_part, 0.0), axis=1)
    rest = col_second - exact_nt(panel0, left_full)
    solved = jax.scipy.linalg.solve_triangular(second_factor, rest.T, lower=True).T
    second_rows = lax.dynamic_slice_in_dim(second_factor, slab_id * quarter, quarter, 0)
    return jnp.where(
        block_id == 0, jnp.zeros_like(solved), jnp.where(block_id == 1, second_rows, solved)
    )


def swap(array, step):
    return lax.ppermute(array, "slab", [(i, i ^ step) for i in range(lax.axis_size("slab"))])


def unscaled_halves(array):
    array = array.astype(jnp.float32) * (1.0 / SOLVE_SCALE)
    high = lax.reduce_precision(array, 8, 7)
    return high.astype(jnp.bfloat16), (array - high).astype(jnp.bfloat16)


def on_device(priv_coeff, priv_var, shared_coeff, shared_var, partners):
    rows = priv_coeff.shape[0]
    blocks, rounds = partners.shape
    block_id = lax.axis_index("blk").astype(jnp.int32)
    slab_id = lax.axis_index("slab").astype(jnp.int32)
    slabs = lax.axis_size("slab")
    quarter = rows // slabs
    place = jnp.stack([block_id, slab_id, slab_id % 2])
    table = partners.T

    pieces, *own_rows = pack(place, shared_coeff, shared_var, blocks, slabs)
    held = lax.all_to_all(pieces, "blk", 0, 0, tiled=True)
    own_rows = [swap(x, step) if step else x for step, x in enumerate(own_rows)]

    partial = partial_diag(place, priv_coeff, priv_var)
    partial, held, own_rows = lax.optimization_barrier((partial, held, own_rows))
    partial = add_shared(place, table, shared_coeff, shared_var, held, partial)
    up, down = DIAG_SCALE, 1.0 / DIAG_SCALE
    near = partial[0] + swap((partial[1] * up).astype(jnp.float16), 1).astype(jnp.float32) * down
    leaving, held = lax.optimization_barrier(((near * up).astype(jnp.float16), held))
    across = swap(leaving, 2)

    mate_coeff = lax.all_to_all(forward(table, held), "blk", 0, 0, tiled=True).reshape(rows, -1)
    cells = SLOT // blocks
    turned = shared_coeff.reshape(rows, rounds, blocks, cells).transpose(2, 1, 3, 0)
    turned = turned.reshape(rounds * SLOT, rows).astype(jnp.float32)
    across, mate_coeff, turned = lax.optimization_barrier((across, mate_coeff, turned))
    mine = near + across.astype(jnp.float32) * down

    from_zero, from_one = partners == 0, partners == 1
    one_each = jnp.logical_not(jnp.any(jnp.any(from_zero, axis=1) & jnp.any(from_one, axis=1)))
    is_coupled = jnp.any(from_zero[1])
    is_simple = one_each & jnp.logical_not(is_coupled)
    later = from_zero[:, 1] | from_one[:, 1]
    zero_later = jnp.where(later, from_zero[:, 1], from_zero[:, 0])
    choice = jnp.where(zero_later, 0, 2) + later.astype(jnp.int32)
    mine, choice, is_simple, is_coupled = lax.optimization_barrier((mine, choice, is_simple, is_coupled))

    other = swap(mine, 1)
    others = [swap(mate_coeff, step) if step else mate_coeff for step in (0, 1, 2)]
    factor_rows, solved = chol_solve(place, mine, other, turned, quarter)
    out = (solved * SOLVE_SCALE).astype(jnp.float16).reshape(blocks, rounds * cells, rows)
    spread_out = lax.all_to_all(out, "blk", 0, 0, tiled=True)
    diag_part = unpack_rows(place, mine, other, rows)
    _, others = lax.optimization_barrier((out, others))
    others = others + [swap(others[2], 1)]
    spread_out, diag_part = lax.optimization_barrier((spread_out, diag_part))

    sources = [spread_out[i, cells * turn : cells * turn + cells] for i in (0, 1) for turn in (0, 1)]
    onward = jnp.broadcast_to(sources[0][None], (blocks, cells, rows))
    for number, source in enumerate(sources[1:], 1):
        onward = jnp.where((choice == number)[:, None, None], source[None], onward)
    arrived = lax.all_to_all(onward, "blk", 0, 0, tiled=True)
    tile_part = pair_tiles(place, table, own_rows, others).reshape(quarter, rounds, rows)
    arrived, tile_part = lax.optimization_barrier((arrived, tile_part))

    def near_half(arrived, kernel):
        beside, across = swap(arrived, 1), swap(arrived, 2)
        highs, lows = zip(*[unscaled_halves(x) for x in (arrived, beside)])
        close = panels(kernel, place, table, own_rows[:2], highs, lows, (factor_rows,))
        across, close = lax.optimization_barrier((across, close))
        highs, lows = zip(*[unscaled_halves(x) for x in (across, swap(across, 1))])
        return highs, lows, close

    highs, lows, close = near_half(arrived.reshape(SLOT, rows), near_chosen_kernel)

    def simple():
        return panels(far_chosen_kernel, place, table, own_rows[2:], highs, lows, close)

    def general():
        wanted = jnp.repeat(from_zero, cells, axis=1)[:, :, None]
        both = jnp.where(wanted, spread_out[0][None], spread_out[1][None])
        both = lax.all_to_all(both, "blk", 0, 0, tiled=True).reshape(blocks, rounds, cells, rows)
        both = both.transpose(1, 0, 2, 3).reshape(solved.shape)
        highs, lows, close = near_half(both, near_kernel)
        panel0, panel1 = panels(far_kernel, place, table, own_rows[2:], highs, lows, close)
        own_row = lax.dynamic_index_in_dim(partners, block_id, 0, False)
        panel1 = lax.cond(
            is_coupled,
            lambda: coupled_panel(panel0, diag_part, tile_part, own_row, block_id, slab_id),
            lambda: panel1,
        )
        return panel0, panel1

    panel0, panel1 = lax.cond(is_simple, simple, general)
    return (diag_part[None], tile_part[None], panel0, panel1)


def solution(mesh):
    in_specs = (P("blk", "slab"), P("blk", "slab"), P("blk", "slab"), P("blk", "slab"), P())
    out_specs = (
        P("blk", "slab", None),
        P("blk", "slab", None, None),
        P(("blk", "slab"), None),
        P(("blk", "slab"), None),
    )
    return jax.shard_map(
        on_device, mesh=mesh, in_specs=in_specs, out_specs=out_specs, check_vma=False
    )
```

```python
import functools

import jax
import jax.numpy as jnp
from jax import lax
from jax.experimental import pallas as pl
from jax.experimental.pallas import tpu as pltpu
from jax.sharding import PartitionSpec as P

SLOT = 128
NB = 128
SUB = 8
BIG = 256
TRIPLE = 16
DEPTH = 512
DIAG_SCALE = 256.0
SOLVE_SCALE = 4096.0
SMEM = pl.BlockSpec(memory_space=pltpu.SMEM)
VMEM = pl.BlockSpec(memory_space=pltpu.VMEM)
NT = (((1,), (1,)), ((), ()))
NN = (((1,), (0,)), ((), ()))


def params():
    return pltpu.CompilerParams(vmem_limit_bytes=48 * 1024 * 1024)


def tri(i, j):
    return i * (i + 1) // 2 + j


def halves(x):
    hi = x.astype(jnp.bfloat16)
    return hi, (x - hi.astype(jnp.float32)).astype(jnp.bfloat16)


def mul(left, right, dims):
    return lax.dot_general(left, right, dims, preferred_element_type=jnp.float32)


def mul3(left, right, dims=NT):
    (lh, ll), (rh, rl) = left, right
    return mul(lh, rh, dims) + (mul(lh, rl, dims) + mul(ll, rh, dims))


def partial_kernel(place_ref, coeff_ref, scale_ref, out_ref):
    per_half, big = out_ref.shape[1], out_ref.shape[2]
    coeff = coeff_ref[...]
    weighted = (coeff.astype(jnp.float32) * scale_ref[...]).astype(jnp.bfloat16)

    def add(first):
        for t, (i, j) in enumerate(packed(coeff.shape[0] // big)):
            part = mul(weighted[big * i : big * i + big], coeff[big * j : big * j + big], NT)
            spot = (t // per_half) ^ place_ref[2]
            if first:
                out_ref[spot, t % per_half] = part
            else:
                out_ref[spot, t % per_half] = out_ref[spot, t % per_half] + part

    @pl.when(pl.program_id(0) == 0)
    def _():
        add(True)

    @pl.when(pl.program_id(0) > 0)
    def _():
        add(False)


def packed(count):
    return [(i, j) for i in range(count) for j in range(i + 1)]


def partial_diag(place, coeff, scale):
    rows, cells = coeff.shape
    depth = min(DEPTH, cells)
    per_half = (rows // BIG) * (rows // BIG + 1) // 4
    shape = (2, per_half, BIG, BIG)
    return pl.pallas_call(
        partial_kernel,
        out_shape=jax.ShapeDtypeStruct(shape, jnp.float32),
        grid=(cells // depth,),
        in_specs=[
            SMEM,
            pl.BlockSpec((rows, depth), lambda k: (0, k)),
            pl.BlockSpec((1, depth), lambda k: (0, k)),
        ],
        out_specs=pl.BlockSpec(shape, lambda k: (0, 0, 0, 0)),
        compiler_params=params(),
        cost_estimate=pl.CostEstimate(
            flops=rows * rows * cells * 2, bytes_accessed=rows * cells * 2, transcendentals=0
        ),
        name="partial_diag",
    )(place, coeff, scale)


def triple_sum(rows):
    rows = rows.astype(jnp.float32)
    return rows[0:1] + rows[1:2] + rows[2:3]


def shared_kernel(place_ref, partners_ref, coeff_ref, own_ref, held_ref, partial_ref, out_ref):
    per_half, big = out_ref.shape[1], out_ref.shape[2]
    blocks, rounds = held_ref.shape[0], held_ref.shape[2] // SLOT
    block, core = place_ref[0], place_ref[2]
    scales = []
    for turn in range(rounds):
        cells = slice(SLOT * turn, SLOT * turn + SLOT)
        listed = partners_ref[turn, block]
        mate = jnp.int32(0)
        for other in range(blocks):
            mate = jnp.where(partners_ref[turn, other] == block, other, mate)
        theirs = triple_sum(held_ref[mate, held_ref.shape[1] - TRIPLE :, cells])
        scales.append(jnp.where(listed >= 0, own_ref[:, cells], theirs))
    scale = jnp.concatenate(scales, axis=1)
    coeff = coeff_ref[...]
    weighted = (coeff.astype(jnp.float32) * scale).astype(jnp.bfloat16)
    for t, (i, j) in enumerate(packed(coeff.shape[0] // big)):
        part = mul(weighted[big * i : big * i + big], coeff[big * j : big * j + big], NT)
        spot = (t // per_half) ^ core
        out_ref[spot, t % per_half] = partial_ref[spot, t % per_half] + part


def add_shared(place, partners, coeff, own_var, held, partial):
    return pl.pallas_call(
        shared_kernel,
        out_shape=jax.ShapeDtypeStruct(partial.shape, jnp.float32),
        in_specs=[SMEM, SMEM, VMEM, VMEM, VMEM, VMEM],
        out_specs=VMEM,
        input_output_aliases={5: 0},
        compiler_params=params(),
        name="add_shared",
    )(place, partners, coeff, own_var, held, partial)


def pack_kernel(place_ref, coeff_ref, var_ref, pieces_ref, *rows_refs):
    chunk = pieces_ref.shape[1] - TRIPLE
    quarter = rows_refs[0].shape[0] - TRIPLE
    var = var_ref[...]
    high = var.astype(jnp.bfloat16).astype(jnp.float32)
    middle = (var - high).astype(jnp.bfloat16).astype(jnp.float32)
    low = var - high - middle
    line = lax.broadcasted_iota(jnp.int32, (TRIPLE, var.shape[1]), 0)
    triple = jnp.where(line == 0, high, jnp.where(line == 1, middle, jnp.where(line == 2, low, 0.0)))
    triple = triple.astype(jnp.bfloat16)
    for block in range(pieces_ref.shape[0]):
        pieces_ref[block, :chunk] = coeff_ref[chunk * block : chunk * block + chunk]
        pieces_ref[block, chunk:] = triple
    for step, rows_ref in enumerate(rows_refs):
        start = pl.multiple_of((place_ref[1] ^ step) * quarter, quarter)
        rows_ref[:quarter] = coeff_ref[pl.ds(start, quarter)]
        rows_ref[quarter:] = triple


def pack(place, coeff, var, blocks, slabs):
    rows, cells = coeff.shape
    return pl.pallas_call(
        pack_kernel,
        out_shape=[jax.ShapeDtypeStruct((blocks, rows // blocks + TRIPLE, cells), coeff.dtype)]
        + [jax.ShapeDtypeStruct((rows // slabs + TRIPLE, cells), coeff.dtype)] * slabs,
        in_specs=[SMEM, VMEM, VMEM],
        out_specs=[VMEM] * (slabs + 1),
        compiler_params=params(),
        name="pack",
    )(place, coeff, var)


def row_bcast(x, j):
    return jnp.broadcast_to(x[j:j+1, :], (SUB, NB))

def col_bcast(x, c):
    return jnp.broadcast_to(x[:, c:c+1], (SUB, NB))

def factor_columns(columns, inverse):
    out = []
    for k in range(SUB):
        column = columns[0] * row_bcast(inverse[0], k)
        for j in range(1, k+1):
            column = column + columns[j] * row_bcast(inverse[j], k)
        out.append(column)
    return out

def factor_tile(tile):
    groups = NB // SUB
    sub = lax.broadcasted_iota(jnp.int32, (SUB, NB), 0)
    lane = lax.broadcasted_iota(jnp.int32, (SUB, NB), 1)
    W = [tile[SUB*g:SUB*g+SUB, :] for g in range(groups)]
    V = [(lane == sub + SUB*g).astype(jnp.float32) for g in range(groups)]
    ups, invs = [], []
    dcol = [col_bcast(W[0], j) for j in range(SUB)]
    left = [col_bcast(W[1], j) for j in range(SUB)]
    right = [col_bcast(W[1], SUB+j) for j in range(SUB)]
    for g in range(groups):
        icol = [(sub == j).astype(jnp.float32) for j in range(SUB)]
        for k in range(SUB):
            r = lax.rsqrt(row_bcast(dcol[k], k))
            lk = dcol[k] * r
            r2 = r * r
            for j in range(k+1, SUB):
                dcol[j] = dcol[j] - (dcol[k] * row_bcast(dcol[k], j)) * r2
            below = jnp.where(sub > k, lk, 0.0)
            for j in range(k+1):
                a = row_bcast(icol[j], k) * r
                icol[j] = jnp.where(sub == k, a, icol[j] - below * a)
        R, S = W[g], V[g]
        U = icol[0] * row_bcast(R, 0)
        SV = icol[0] * row_bcast(S, 0)
        for j in range(1, SUB):
            U = U + icol[j] * row_bcast(R, j)
            SV = SV + icol[j] * row_bcast(S, j)
        U = jnp.where(lane >= sub + SUB*g, U, 0.0)
        ups.append(U); invs.append(SV)
        if g + 1 == groups:
            break
        first = factor_columns(left, icol)
        dcol = right
        for k in range(SUB):
            for j in range(SUB):
                dcol[j] = dcol[j] - first[k] * row_bcast(first[k], j)
            W[g+1] = W[g+1] - first[k] * row_bcast(U, k)
            V[g+1] = V[g+1] - first[k] * row_bcast(SV, k)
        if g + 2 == groups:
            continue
        second = factor_columns([col_bcast(W[g+2], SUB*g+j) for j in range(SUB)], icol)
        left = [col_bcast(W[g+2], SUB*(g+1)+j) for j in range(SUB)]
        right = [col_bcast(W[g+2], SUB*(g+2)+j) for j in range(SUB)]
        for k in range(SUB):
            for j in range(SUB):
                left[j] = left[j] - second[k] * row_bcast(first[k], j)
                right[j] = right[j] - second[k] * row_bcast(second[k], j)
            W[g+2] = W[g+2] - second[k] * row_bcast(U, k)
            V[g+2] = V[g+2] - second[k] * row_bcast(SV, k)
        if g + 3 < groups:
            uh = U.astype(jnp.bfloat16).astype(jnp.float32)
            ul = U - uh
            sh = SV.astype(jnp.bfloat16).astype(jnp.float32)
            sl = SV - sh
            zero = jnp.zeros((SUB, NB), jnp.float32)
            lhs = jnp.concatenate([uh, ul, uh, zero], 0).astype(jnp.bfloat16)
            rhs = jnp.concatenate([
                jnp.concatenate([uh, uh, ul, zero], 0),
                jnp.concatenate([sh, sh, sl, zero], 0)], 1).astype(jnp.bfloat16)
            upd = lax.dot_general(lhs, rhs, (((0,), (0,)), ((), ())), preferred_element_type=jnp.float32)
            for t in range(g+3, groups):
                W[t] = W[t] - upd[SUB*t:SUB*t+SUB, :NB]
                V[t] = V[t] - upd[SUB*t:SUB*t+SUB, NB:]
    return jnp.concatenate(ups, 0), jnp.concatenate(invs, 0)


def chol_kernel(place_ref, mine_ref, other_ref, ct_ref, lrow_ref, zt_ref, M):
    n = zt_ref.shape[1]
    cb = n // NB
    extra = ct_ref.shape[0]
    total = n + extra
    quarter = lrow_ref.shape[0]
    big = mine_ref.shape[1]
    nbig = n // big
    half = mine_ref.shape[0]
    per = big // NB
    is0 = place_ref[2] == 0
    for i in range(nbig):
        for j in range(i+1):
            t = tri(i, j)
            if t < half:
                x = jnp.where(is0, mine_ref[t], other_ref[t])
            else:
                x = jnp.where(is0, other_ref[t-half], mine_ref[t-half])
            for b in range(per):
                M[j*per+b, big*i:big*i+big, :] = x[:, NB*b:NB*b+NB]
    for q in range(cb):
        M[q, n:total, :] = ct_ref[:, NB*q:NB*q+NB]

    def step_rest(p, inv):
        inv_parts = halves(inv)
        lo = (p+1)*NB
        below = mul3(halves(M[p, lo:total, :]), inv_parts)
        M[p, lo:total, :] = below
        high, low = halves(below)
        q = p + 1
        while q < cb:
            w = 1
            a = (q - p - 1)*NB
            acc = mul3((high[a:], low[a:]), (high[a:a+w*NB], low[a:a+w*NB]))
            for b in range(w):
                M[q+b, q*NB:total, :] = M[q+b, q*NB:total, :] - acc[:, b*NB:b*NB+NB]
            q += w

    def body(p, carry):
        rows = pl.ds(pl.multiple_of(p*NB, NB), NB)
        up, inv = factor_tile(M[p, rows, :])
        M[p, rows, :] = up.T
        for s in range(cb):
            @pl.when(p == s)
            def _():
                step_rest(s, inv)
        return carry
    lax.fori_loop(0, cb, body, 0)
    start = pl.multiple_of(place_ref[1]*quarter, quarter)
    ids = lax.broadcasted_iota(jnp.int32, (quarter, NB), 0) + start
    for q in range(cb):
        lrow_ref[:, NB*q:NB*q+NB] = jnp.where(ids >= q*NB, M[q, pl.ds(start, quarter), :], 0.0)
        zt_ref[:, NB*q:NB*q+NB] = M[q, n:total, :]

def chol_solve(place, mine, other, ct, quarter):
    n = ct.shape[1]
    extra = ct.shape[0]
    return pl.pallas_call(
        chol_kernel,
        out_shape=(jax.ShapeDtypeStruct((quarter, n), jnp.float32), jax.ShapeDtypeStruct((extra, n), jnp.float32)),
        in_specs=[SMEM, VMEM, VMEM, VMEM],
        out_specs=(VMEM, VMEM),
        scratch_shapes=[pltpu.VMEM((n//NB, n+extra, NB), jnp.float32)],
        compiler_params=params(),
        cost_estimate=pl.CostEstimate(flops=40 * 10**9, bytes_accessed=8 * n * n, transcendentals=0),
        name="factor_solve",
    )(place, mine, other, ct)


def unpack_kernel(place_ref, mine_ref, other_ref, out_ref):
    per_half, big = mine_ref.shape[0], mine_ref.shape[1]
    row = place_ref[1]
    for t in range(out_ref.shape[1] // big):
        high, low = jnp.maximum(row, t), jnp.minimum(row, t)
        spot = high * (high + 1) // 2 + low
        upper = (spot >= per_half).astype(jnp.int32)
        slot = spot - upper * per_half
        tile = jnp.where(upper == place_ref[2], mine_ref[slot], other_ref[slot])
        out_ref[:, big * t : big * t + big] = jnp.where(row < t, tile.T, tile)


def unpack_rows(place, mine, other, rows):
    return pl.pallas_call(
        unpack_kernel,
        out_shape=jax.ShapeDtypeStruct((mine.shape[1], rows), jnp.float32),
        in_specs=[SMEM, VMEM, VMEM],
        out_specs=VMEM,
        compiler_params=params(),
        name="diag_rows",
    )(place, mine, other)


def forward_kernel(partners_ref, held_ref, out_ref):
    blocks, chunk, cells = out_ref.shape
    rounds = cells // SLOT
    for block in range(blocks):
        for turn in range(rounds):
            source = jnp.maximum(partners_ref[turn, block], 0)
            columns = slice(SLOT * turn, SLOT * turn + SLOT)
            out_ref[block, :, columns] = held_ref[source, :chunk, columns]


def forward(partners, held):
    return pl.pallas_call(
        forward_kernel,
        out_shape=jax.ShapeDtypeStruct((held.shape[0], held.shape[1] - TRIPLE, held.shape[2]), held.dtype),
        in_specs=[SMEM, VMEM],
        out_specs=VMEM,
        compiler_params=params(),
        name="forward",
    )(partners, held)


def row_weights(row_refs, cells):
    pieces = []
    for ref in row_refs:
        quarter = ref.shape[0] - TRIPLE
        pieces.append(ref[:quarter, cells].astype(jnp.float32) * triple_sum(ref[quarter:, cells]))
    return halves(jnp.concatenate(pieces, axis=1))


def tiles_kernel(place_ref, partners_ref, *refs):
    row_refs, other_refs, out_ref = refs[:4], refs[4:8], refs[8]
    rows, rounds = other_refs[0].shape[0], other_refs[0].shape[1] // SLOT
    for turn in range(rounds):
        cells = slice(SLOT * turn, SLOT * turn + SLOT)
        high, low = row_weights(row_refs, cells)
        other = jnp.concatenate([x[:, cells] for x in other_refs], axis=1)
        tile = mul(high, other, NT) + mul(low, other, NT)
        listed = partners_ref[turn, place_ref[0]] >= 0
        out_ref[:, rows * turn : rows * turn + rows] = jnp.where(listed, tile, 0.0)


def pair_tiles(place, partners, own_rows, others):
    quarter, (rows, cells) = own_rows[0].shape[0] - TRIPLE, others[0].shape
    return pl.pallas_call(
        tiles_kernel,
        out_shape=jax.ShapeDtypeStruct((quarter, cells // SLOT * rows), jnp.float32),
        in_specs=[SMEM, SMEM] + [VMEM] * 8,
        out_specs=VMEM,
        compiler_params=params(),
        cost_estimate=pl.CostEstimate(flops=3 * 10**9, bytes_accessed=5 * 10**6, transcendentals=0),
        name="pair_tiles",
    )(place, partners, *own_rows, *others)


def solved_sum(place_ref, partners_ref, row_refs, high_refs, low_refs):
    rounds = row_refs[0].shape[1] // SLOT
    first, second = 0.0, 0.0
    for turn in range(rounds):
        cells = slice(SLOT * turn, SLOT * turn + SLOT)
        high = jnp.concatenate([x[cells, :] for x in high_refs], axis=0)
        low = jnp.concatenate([x[cells, :] for x in low_refs], axis=0)
        solved = mul3(row_weights(row_refs, cells), (high, low), NN)
        listed = partners_ref[turn, place_ref[0]]
        first = first + jnp.where(listed == 0, solved, 0.0)
        second = second + jnp.where(listed == 1, solved, 0.0)
    return first, second


def near_kernel(place_ref, partners_ref, *refs):
    factor_ref, zero_ref, one_ref = refs[6:]
    first, second = solved_sum(place_ref, partners_ref, refs[:2], refs[2:4], refs[4:6])
    zero_ref[...] = jnp.where(place_ref[0] == 0, factor_ref[...], first)
    one_ref[...] = jnp.where(place_ref[0] == 1, factor_ref[...], second)


def far_kernel(place_ref, partners_ref, *refs):
    near_zero_ref, near_one_ref, zero_ref, one_ref = refs[6:]
    first, second = solved_sum(place_ref, partners_ref, refs[:2], refs[2:4], refs[4:6])
    zero_ref[...] = near_zero_ref[...] + jnp.where(place_ref[0] == 0, 0.0, first)
    one_ref[...] = near_one_ref[...] + jnp.where(place_ref[0] == 1, 0.0, second)


def chosen_sum(place_ref, partners_ref, row_refs, high_refs, low_refs):
    block = place_ref[0]
    later = partners_ref[1, block]
    is_later = jnp.logical_or(later == 0, later == 1)
    listed = jnp.where(is_later, later, partners_ref[0, block])
    pieces = []
    for ref in row_refs:
        quarter = ref.shape[0] - TRIPLE
        parts = []
        for turn in range(2):
            cells = slice(SLOT * turn, SLOT * turn + SLOT)
            parts.append(ref[:quarter, cells].astype(jnp.float32) * triple_sum(ref[quarter:, cells]))
        pieces.append(jnp.where(is_later, parts[1], parts[0]))
    weight = halves(jnp.concatenate(pieces, axis=1))
    high = jnp.concatenate([x[...] for x in high_refs], axis=0)
    low = jnp.concatenate([x[...] for x in low_refs], axis=0)
    solved = mul3(weight, (high, low), NN)
    return jnp.where(listed == 0, solved, 0.0), jnp.where(listed == 1, solved, 0.0)


def near_chosen_kernel(place_ref, partners_ref, *refs):
    factor_ref, zero_ref, one_ref = refs[6:]
    first, second = chosen_sum(place_ref, partners_ref, refs[:2], refs[2:4], refs[4:6])
    zero_ref[...] = jnp.where(place_ref[0] == 0, factor_ref[...], first)
    one_ref[...] = jnp.where(place_ref[0] == 1, factor_ref[...], second)


def far_chosen_kernel(place_ref, partners_ref, *refs):
    near_zero_ref, near_one_ref, zero_ref, one_ref = refs[6:]
    first, second = chosen_sum(place_ref, partners_ref, refs[:2], refs[2:4], refs[4:6])
    zero_ref[...] = near_zero_ref[...] + jnp.where(place_ref[0] == 0, 0.0, first)
    one_ref[...] = near_one_ref[...] + jnp.where(place_ref[0] == 1, 0.0, second)


def panels(kernel, place, partners, own_rows, highs, lows, more):
    shape = jax.ShapeDtypeStruct((own_rows[0].shape[0] - TRIPLE, highs[0].shape[1]), jnp.float32)
    return pl.pallas_call(
        kernel,
        out_shape=(shape, shape),
        in_specs=[SMEM, SMEM] + [VMEM] * (6 + len(more)),
        out_specs=(VMEM, VMEM),
        compiler_params=params(),
        cost_estimate=pl.CostEstimate(flops=3 * 10**9, bytes_accessed=5 * 10**6, transcendentals=0),
        name=kernel.__name__[:-7] + "_panels",
    )(place, partners, *own_rows, *highs, *lows, *more)


def spread(array, axis, root):
    mine = lax.axis_index(axis) == root
    return lax.psum(jnp.where(mine, array, jnp.zeros_like(array)), axis)


def exact_nt(left, right):
    return lax.dot_general(
        left, right, NT, precision=lax.Precision.HIGHEST, preferred_element_type=jnp.float32
    )


def coupled_panel(panel0, diag_part, tile_part, own_row, block_id, slab_id):
    quarter = panel0.shape[0]
    left_part, second_part = spread(panel0, "blk", 1), spread(diag_part, "blk", 1)
    left_full = lax.all_gather(left_part, "slab", axis=0, tiled=True)
    second_full = lax.all_gather(second_part, "slab", axis=0, tiled=True)
    second_factor = jnp.linalg.cholesky(second_full - exact_nt(left_full, left_full))
    col_second = jnp.sum(jnp.where((own_row == 1)[None, :, None], tile_part, 0.0), axis=1)
    rest = col_second - exact_nt(panel0, left_full)
    solved = jax.scipy.linalg.solve_triangular(second_factor, rest.T, lower=True).T
    second_rows = lax.dynamic_slice_in_dim(second_factor, slab_id * quarter, quarter, 0)
    return jnp.where(
        block_id == 0, jnp.zeros_like(solved), jnp.where(block_id == 1, second_rows, solved)
    )


def swap(array, step):
    return lax.ppermute(array, "slab", [(i, i ^ step) for i in range(lax.axis_size("slab"))])


def unscaled_halves(array):
    array = array.astype(jnp.float32) * (1.0 / SOLVE_SCALE)
    high = lax.reduce_precision(array, 8, 7)
    return high.astype(jnp.bfloat16), (array - high).astype(jnp.bfloat16)


def on_device(priv_coeff, priv_var, shared_coeff, shared_var, partners):
    rows = priv_coeff.shape[0]
    blocks, rounds = partners.shape
    block_id = lax.axis_index("blk").astype(jnp.int32)
    slab_id = lax.axis_index("slab").astype(jnp.int32)
    slabs = lax.axis_size("slab")
    quarter = rows // slabs
    place = jnp.stack([block_id, slab_id, slab_id % 2])
    table = partners.T

    pieces, *own_rows = pack(place, shared_coeff, shared_var, blocks, slabs)
    held = lax.all_to_all(pieces, "blk", 0, 0, tiled=True)
    own_rows = [swap(x, step) if step else x for step, x in enumerate(own_rows)]

    partial = partial_diag(place, priv_coeff, priv_var)
    partial, held, own_rows = lax.optimization_barrier((partial, held, own_rows))
    partial = add_shared(place, table, shared_coeff, shared_var, held, partial)
    up, down = DIAG_SCALE, 1.0 / DIAG_SCALE
    near = partial[0] + swap((partial[1] * up).astype(jnp.float16), 1).astype(jnp.float32) * down
    leaving, held = lax.optimization_barrier(((near * up).astype(jnp.float16), held))
    across = swap(leaving, 2)

    mate_coeff = lax.all_to_all(forward(table, held), "blk", 0, 0, tiled=True).reshape(rows, -1)
    cells = SLOT // blocks
    turned = shared_coeff.reshape(rows, rounds, blocks, cells).transpose(2, 1, 3, 0)
    turned = turned.reshape(rounds * SLOT, rows).astype(jnp.float32)
    across, mate_coeff, turned = lax.optimization_barrier((across, mate_coeff, turned))
    mine = near + across.astype(jnp.float32) * down

    from_zero, from_one = partners == 0, partners == 1
    one_each = jnp.logical_not(jnp.any(jnp.any(from_zero, axis=1) & jnp.any(from_one, axis=1)))
    is_coupled = jnp.any(from_zero[1])
    is_simple = one_each & jnp.logical_not(is_coupled)
    later = from_zero[:, 1] | from_one[:, 1]
    zero_later = jnp.where(later, from_zero[:, 1], from_zero[:, 0])
    choice = jnp.where(zero_later, 0, 2) + later.astype(jnp.int32)
    mine, choice, is_simple, is_coupled = lax.optimization_barrier((mine, choice, is_simple, is_coupled))

    other = swap(mine, 1)
    others = [swap(mate_coeff, step) if step else mate_coeff for step in (0, 1, 2)]
    factor_rows, solved = chol_solve(place, mine, other, turned, quarter)
    out = (solved * SOLVE_SCALE).astype(jnp.float16).reshape(blocks, rounds * cells, rows)
    spread_out = lax.all_to_all(out, "blk", 0, 0, tiled=True)
    diag_part = unpack_rows(place, mine, other, rows)
    _, others = lax.optimization_barrier((out, others))
    others = others + [swap(others[2], 1)]
    spread_out, diag_part = lax.optimization_barrier((spread_out, diag_part))

    sources = [spread_out[i, cells * turn : cells * turn + cells] for i in (0, 1) for turn in (0, 1)]
    onward = jnp.broadcast_to(sources[0][None], (blocks, cells, rows))
    for number, source in enumerate(sources[1:], 1):
        onward = jnp.where((choice == number)[:, None, None], source[None], onward)
    arrived = lax.all_to_all(onward, "blk", 0, 0, tiled=True)
    tile_part = pair_tiles(place, table, own_rows, others).reshape(quarter, rounds, rows)
    arrived, tile_part = lax.optimization_barrier((arrived, tile_part))

    def near_half(arrived, kernel):
        beside, across = swap(arrived, 1), swap(arrived, 2)
        highs, lows = zip(*[unscaled_halves(x) for x in (arrived, beside)])
        close = panels(kernel, place, table, own_rows[:2], highs, lows, (factor_rows,))
        across, close = lax.optimization_barrier((across, close))
        highs, lows = zip(*[unscaled_halves(x) for x in (across, swap(across, 1))])
        return highs, lows, close

    highs, lows, close = near_half(arrived.reshape(SLOT, rows), near_chosen_kernel)

    def simple():
        return panels(far_chosen_kernel, place, table, own_rows[2:], highs, lows, close)

    def general():
        wanted = jnp.repeat(from_zero, cells, axis=1)[:, :, None]
        both = jnp.where(wanted, spread_out[0][None], spread_out[1][None])
        both = lax.all_to_all(both, "blk", 0, 0, tiled=True).reshape(blocks, rounds, cells, rows)
        both = both.transpose(1, 0, 2, 3).reshape(solved.shape)
        highs, lows, close = near_half(both, near_kernel)
        panel0, panel1 = panels(far_kernel, place, table, own_rows[2:], highs, lows, close)
        own_row = lax.dynamic_index_in_dim(partners, block_id, 0, False)
        panel1 = lax.cond(
            is_coupled,
            lambda: coupled_panel(panel0, diag_part, tile_part, own_row, block_id, slab_id),
            lambda: panel1,
        )
        return panel0, panel1

    panel0, panel1 = lax.cond(is_simple, simple, general)
    return (diag_part[None], tile_part[None], panel0, panel1)


def solution(mesh):
    in_specs = (P("blk", "slab"), P("blk", "slab"), P("blk", "slab"), P("blk", "slab"), P())
    out_specs = (
        P("blk", "slab", None),
        P("blk", "slab", None, None),
        P(("blk", "slab"), None),
        P(("blk", "slab"), None),
    )
    return jax.shard_map(
        on_device, mesh=mesh, in_specs=in_specs, out_specs=out_specs, check_vma=False
    )
```

```python
import functools

import jax
import jax.numpy as jnp
from jax import lax
from jax.experimental import pallas as pl
from jax.experimental.pallas import tpu as pltpu
from jax.sharding import PartitionSpec as P

SLOT = 128
NB = 128
SUB = 8
BIG = 256
TRIPLE = 16
DEPTH = 1024
DIAG_SCALE = 256.0
SOLVE_SCALE = 4096.0
SMEM = pl.BlockSpec(memory_space=pltpu.SMEM)
VMEM = pl.BlockSpec(memory_space=pltpu.VMEM)
NT = (((1,), (1,)), ((), ()))
NN = (((1,), (0,)), ((), ()))


def params():
    return pltpu.CompilerParams(vmem_limit_bytes=48 * 1024 * 1024)


def tri(i, j):
    return i * (i + 1) // 2 + j


def halves(x):
    hi = x.astype(jnp.bfloat16)
    return hi, (x - hi.astype(jnp.float32)).astype(jnp.bfloat16)


def mul(left, right, dims):
    return lax.dot_general(left, right, dims, preferred_element_type=jnp.float32)


def mul3(left, right, dims=NT):
    (lh, ll), (rh, rl) = left, right
    return mul(lh, rh, dims) + (mul(lh, rl, dims) + mul(ll, rh, dims))


def partial_kernel(place_ref, coeff_ref, scale_ref, out_ref):
    per_half, big = out_ref.shape[1], out_ref.shape[2]
    coeff = coeff_ref[...]
    weighted = (coeff.astype(jnp.float32) * scale_ref[...]).astype(jnp.bfloat16)

    def add(first):
        for t, (i, j) in enumerate(packed(coeff.shape[0] // big)):
            part = mul(weighted[big * i : big * i + big], coeff[big * j : big * j + big], NT)
            spot = (t // per_half) ^ place_ref[2]
            if first:
                out_ref[spot, t % per_half] = part
            else:
                out_ref[spot, t % per_half] = out_ref[spot, t % per_half] + part

    @pl.when(pl.program_id(0) == 0)
    def _():
        add(True)

    @pl.when(pl.program_id(0) > 0)
    def _():
        add(False)


def packed(count):
    return [(i, j) for i in range(count) for j in range(i + 1)]


def partial_diag(place, coeff, scale):
    rows, cells = coeff.shape
    depth = min(DEPTH, cells)
    per_half = (rows // BIG) * (rows // BIG + 1) // 4
    shape = (2, per_half, BIG, BIG)
    return pl.pallas_call(
        partial_kernel,
        out_shape=jax.ShapeDtypeStruct(shape, jnp.float32),
        grid=(cells // depth,),
        in_specs=[
            SMEM,
            pl.BlockSpec((rows, depth), lambda k: (0, k)),
            pl.BlockSpec((1, depth), lambda k: (0, k)),
        ],
        out_specs=pl.BlockSpec(shape, lambda k: (0, 0, 0, 0)),
        compiler_params=params(),
        cost_estimate=pl.CostEstimate(
            flops=rows * rows * cells * 2, bytes_accessed=rows * cells * 2, transcendentals=0
        ),
        name="partial_diag",
    )(place, coeff, scale)


def triple_sum(rows):
    rows = rows.astype(jnp.float32)
    return rows[0:1] + rows[1:2] + rows[2:3]


def shared_kernel(place_ref, partners_ref, coeff_ref, own_ref, held_ref, partial_ref, out_ref):
    per_half, big = out_ref.shape[1], out_ref.shape[2]
    blocks, rounds = held_ref.shape[0], held_ref.shape[2] // SLOT
    block, core = place_ref[0], place_ref[2]
    scales = []
    for turn in range(rounds):
        cells = slice(SLOT * turn, SLOT * turn + SLOT)
        listed = partners_ref[turn, block]
        mate = jnp.int32(0)
        for other in range(blocks):
            mate = jnp.where(partners_ref[turn, other] == block, other, mate)
        theirs = triple_sum(held_ref[mate, held_ref.shape[1] - TRIPLE :, cells])
        scales.append(jnp.where(listed >= 0, own_ref[:, cells], theirs))
    scale = jnp.concatenate(scales, axis=1)
    coeff = coeff_ref[...]
    weighted = (coeff.astype(jnp.float32) * scale).astype(jnp.bfloat16)
    for t, (i, j) in enumerate(packed(coeff.shape[0] // big)):
        part = mul(weighted[big * i : big * i + big], coeff[big * j : big * j + big], NT)
        spot = (t // per_half) ^ core
        out_ref[spot, t % per_half] = partial_ref[spot, t % per_half] + part


def add_shared(place, partners, coeff, own_var, held, partial):
    return pl.pallas_call(
        shared_kernel,
        out_shape=jax.ShapeDtypeStruct(partial.shape, jnp.float32),
        in_specs=[SMEM, SMEM, VMEM, VMEM, VMEM, VMEM],
        out_specs=VMEM,
        input_output_aliases={5: 0},
        compiler_params=params(),
        name="add_shared",
    )(place, partners, coeff, own_var, held, partial)


def pack_kernel(place_ref, coeff_ref, var_ref, pieces_ref, *rows_refs):
    chunk = pieces_ref.shape[1] - TRIPLE
    quarter = rows_refs[0].shape[0] - TRIPLE
    var = var_ref[...]
    high = var.astype(jnp.bfloat16).astype(jnp.float32)
    middle = (var - high).astype(jnp.bfloat16).astype(jnp.float32)
    low = var - high - middle
    line = lax.broadcasted_iota(jnp.int32, (TRIPLE, var.shape[1]), 0)
    triple = jnp.where(line == 0, high, jnp.where(line == 1, middle, jnp.where(line == 2, low, 0.0)))
    triple = triple.astype(jnp.bfloat16)
    for block in range(pieces_ref.shape[0]):
        pieces_ref[block, :chunk] = coeff_ref[chunk * block : chunk * block + chunk]
        pieces_ref[block, chunk:] = triple
    for step, rows_ref in enumerate(rows_refs):
        start = pl.multiple_of((place_ref[1] ^ step) * quarter, quarter)
        rows_ref[:quarter] = coeff_ref[pl.ds(start, quarter)]
        rows_ref[quarter:] = triple


def pack(place, coeff, var, blocks, slabs):
    rows, cells = coeff.shape
    return pl.pallas_call(
        pack_kernel,
        out_shape=[jax.ShapeDtypeStruct((blocks, rows // blocks + TRIPLE, cells), coeff.dtype)]
        + [jax.ShapeDtypeStruct((rows // slabs + TRIPLE, cells), coeff.dtype)] * slabs,
        in_specs=[SMEM, VMEM, VMEM],
        out_specs=[VMEM] * (slabs + 1),
        compiler_params=params(),
        name="pack",
    )(place, coeff, var)


def row_bcast(x, j):
    return jnp.broadcast_to(x[j:j+1, :], (SUB, NB))

def col_bcast(x, c):
    return jnp.broadcast_to(x[:, c:c+1], (SUB, NB))

def factor_columns(columns, inverse):
    out = []
    for k in range(SUB):
        column = columns[0] * row_bcast(inverse[0], k)
        for j in range(1, k+1):
            column = column + columns[j] * row_bcast(inverse[j], k)
        out.append(column)
    return out

def factor_tile(tile):
    groups = NB // SUB
    sub = lax.broadcasted_iota(jnp.int32, (SUB, NB), 0)
    lane = lax.broadcasted_iota(jnp.int32, (SUB, NB), 1)
    W = [tile[SUB*g:SUB*g+SUB, :] for g in range(groups)]
    V = [(lane == sub + SUB*g).astype(jnp.float32) for g in range(groups)]
    ups, invs = [], []
    dcol = [col_bcast(W[0], j) for j in range(SUB)]
    left = [col_bcast(W[1], j) for j in range(SUB)]
    right = [col_bcast(W[1], SUB+j) for j in range(SUB)]
    for g in range(groups):
        icol = [(sub == j).astype(jnp.float32) for j in range(SUB)]
        for k in range(SUB):
            r = lax.rsqrt(row_bcast(dcol[k], k))
            lk = dcol[k] * r
            r2 = r * r
            for j in range(k+1, SUB):
                dcol[j] = dcol[j] - (dcol[k] * row_bcast(dcol[k], j)) * r2
            below = jnp.where(sub > k, lk, 0.0)
            for j in range(k+1):
                a = row_bcast(icol[j], k) * r
                icol[j] = jnp.where(sub == k, a, icol[j] - below * a)
        R, S = W[g], V[g]
        U = icol[0] * row_bcast(R, 0)
        SV = icol[0] * row_bcast(S, 0)
        for j in range(1, SUB):
            U = U + icol[j] * row_bcast(R, j)
            SV = SV + icol[j] * row_bcast(S, j)
        U = jnp.where(lane >= sub + SUB*g, U, 0.0)
        ups.append(U); invs.append(SV)
        if g + 1 == groups:
            break
        first = factor_columns(left, icol)
        dcol = right
        for k in range(SUB):
            for j in range(SUB):
                dcol[j] = dcol[j] - first[k] * row_bcast(first[k], j)
            W[g+1] = W[g+1] - first[k] * row_bcast(U, k)
            V[g+1] = V[g+1] - first[k] * row_bcast(SV, k)
        if g + 2 == groups:
            continue
        second = factor_columns([col_bcast(W[g+2], SUB*g+j) for j in range(SUB)], icol)
        left = [col_bcast(W[g+2], SUB*(g+1)+j) for j in range(SUB)]
        right = [col_bcast(W[g+2], SUB*(g+2)+j) for j in range(SUB)]
        for k in range(SUB):
            for j in range(SUB):
                left[j] = left[j] - second[k] * row_bcast(first[k], j)
                right[j] = right[j] - second[k] * row_bcast(second[k], j)
            W[g+2] = W[g+2] - second[k] * row_bcast(U, k)
            V[g+2] = V[g+2] - second[k] * row_bcast(SV, k)
        if g + 3 < groups:
            uh = U.astype(jnp.bfloat16).astype(jnp.float32)
            ul = U - uh
            sh = SV.astype(jnp.bfloat16).astype(jnp.float32)
            sl = SV - sh
            zero = jnp.zeros((SUB, NB), jnp.float32)
            lhs = jnp.concatenate([uh, ul, uh, zero], 0).astype(jnp.bfloat16)
            rhs = jnp.concatenate([
                jnp.concatenate([uh, uh, ul, zero], 0),
                jnp.concatenate([sh, sh, sl, zero], 0)], 1).astype(jnp.bfloat16)
            upd = lax.dot_general(lhs, rhs, (((0,), (0,)), ((), ())), preferred_element_type=jnp.float32)
            for t in range(g+3, groups):
                W[t] = W[t] - upd[SUB*t:SUB*t+SUB, :NB]
                V[t] = V[t] - upd[SUB*t:SUB*t+SUB, NB:]
    return jnp.concatenate(ups, 0), jnp.concatenate(invs, 0)


def chol_kernel(place_ref, mine_ref, other_ref, ct_ref, lrow_ref, zt_ref, M):
    n = zt_ref.shape[1]
    cb = n // NB
    extra = ct_ref.shape[0]
    total = n + extra
    quarter = lrow_ref.shape[0]
    big = mine_ref.shape[1]
    nbig = n // big
    half = mine_ref.shape[0]
    per = big // NB
    is0 = place_ref[2] == 0
    for i in range(nbig):
        for j in range(i+1):
            t = tri(i, j)
            if t < half:
                x = jnp.where(is0, mine_ref[t], other_ref[t])
            else:
                x = jnp.where(is0, other_ref[t-half], mine_ref[t-half])
            for b in range(per):
                M[j*per+b, big*i:big*i+big, :] = x[:, NB*b:NB*b+NB]
    for q in range(cb):
        M[q, n:total, :] = ct_ref[:, NB*q:NB*q+NB]

    def step_rest(p, inv):
        inv_parts = halves(inv)
        lo = (p+1)*NB
        below = mul3(halves(M[p, lo:total, :]), inv_parts)
        M[p, lo:total, :] = below
        high, low = halves(below)
        q = p + 1
        while q < cb:
            w = 1
            a = (q - p - 1)*NB
            acc = mul3((high[a:], low[a:]), (high[a:a+w*NB], low[a:a+w*NB]))
            for b in range(w):
                M[q+b, q*NB:total, :] = M[q+b, q*NB:total, :] - acc[:, b*NB:b*NB+NB]
            q += w

    def body(p, carry):
        rows = pl.ds(pl.multiple_of(p*NB, NB), NB)
        up, inv = factor_tile(M[p, rows, :])
        M[p, rows, :] = up.T
        for s in range(cb):
            @pl.when(p == s)
            def _():
                step_rest(s, inv)
        return carry
    lax.fori_loop(0, cb, body, 0)
    start = pl.multiple_of(place_ref[1]*quarter, quarter)
    ids = lax.broadcasted_iota(jnp.int32, (quarter, NB), 0) + start
    for q in range(cb):
        lrow_ref[:, NB*q:NB*q+NB] = jnp.where(ids >= q*NB, M[q, pl.ds(start, quarter), :], 0.0)
        zt_ref[:, NB*q:NB*q+NB] = M[q, n:total, :]

def chol_solve(place, mine, other, ct, quarter):
    n = ct.shape[1]
    extra = ct.shape[0]
    return pl.pallas_call(
        chol_kernel,
        out_shape=(jax.ShapeDtypeStruct((quarter, n), jnp.float32), jax.ShapeDtypeStruct((extra, n), jnp.float32)),
        in_specs=[SMEM, VMEM, VMEM, VMEM],
        out_specs=(VMEM, VMEM),
        scratch_shapes=[pltpu.VMEM((n//NB, n+extra, NB), jnp.float32)],
        compiler_params=params(),
        cost_estimate=pl.CostEstimate(flops=40 * 10**9, bytes_accessed=8 * n * n, transcendentals=0),
        name="factor_solve",
    )(place, mine, other, ct)


def unpack_kernel(place_ref, mine_ref, other_ref, out_ref):
    per_half, big = mine_ref.shape[0], mine_ref.shape[1]
    row = place_ref[1]
    for t in range(out_ref.shape[1] // big):
        high, low = jnp.maximum(row, t), jnp.minimum(row, t)
        spot = high * (high + 1) // 2 + low
        upper = (spot >= per_half).astype(jnp.int32)
        slot = spot - upper * per_half
        tile = jnp.where(upper == place_ref[2], mine_ref[slot], other_ref[slot])
        out_ref[:, big * t : big * t + big] = jnp.where(row < t, tile.T, tile)


def unpack_rows(place, mine, other, rows):
    return pl.pallas_call(
        unpack_kernel,
        out_shape=jax.ShapeDtypeStruct((mine.shape[1], rows), jnp.float32),
        in_specs=[SMEM, VMEM, VMEM],
        out_specs=VMEM,
        compiler_params=params(),
        name="diag_rows",
    )(place, mine, other)


def forward_kernel(partners_ref, held_ref, out_ref):
    blocks, chunk, cells = out_ref.shape
    rounds = cells // SLOT
    for block in range(blocks):
        for turn in range(rounds):
            source = jnp.maximum(partners_ref[turn, block], 0)
            columns = slice(SLOT * turn, SLOT * turn + SLOT)
            out_ref[block, :, columns] = held_ref[source, :chunk, columns]


def forward(partners, held):
    return pl.pallas_call(
        forward_kernel,
        out_shape=jax.ShapeDtypeStruct((held.shape[0], held.shape[1] - TRIPLE, held.shape[2]), held.dtype),
        in_specs=[SMEM, VMEM],
        out_specs=VMEM,
        compiler_params=params(),
        name="forward",
    )(partners, held)


def row_weights(row_refs, cells):
    pieces = []
    for ref in row_refs:
        quarter = ref.shape[0] - TRIPLE
        pieces.append(ref[:quarter, cells].astype(jnp.float32) * triple_sum(ref[quarter:, cells]))
    return halves(jnp.concatenate(pieces, axis=1))


def tiles_kernel(place_ref, partners_ref, *refs):
    row_refs, other_refs, out_ref = refs[:4], refs[4:8], refs[8]
    rows, rounds = other_refs[0].shape[0], other_refs[0].shape[1] // SLOT
    for turn in range(rounds):
        cells = slice(SLOT * turn, SLOT * turn + SLOT)
        high, low = row_weights(row_refs, cells)
        other = jnp.concatenate([x[:, cells] for x in other_refs], axis=1)
        tile = mul(high, other, NT) + mul(low, other, NT)
        listed = partners_ref[turn, place_ref[0]] >= 0
        out_ref[:, rows * turn : rows * turn + rows] = jnp.where(listed, tile, 0.0)


def pair_tiles(place, partners, own_rows, others):
    quarter, (rows, cells) = own_rows[0].shape[0] - TRIPLE, others[0].shape
    return pl.pallas_call(
        tiles_kernel,
        out_shape=jax.ShapeDtypeStruct((quarter, cells // SLOT * rows), jnp.float32),
        in_specs=[SMEM, SMEM] + [VMEM] * 8,
        out_specs=VMEM,
        compiler_params=params(),
        cost_estimate=pl.CostEstimate(flops=3 * 10**9, bytes_accessed=5 * 10**6, transcendentals=0),
        name="pair_tiles",
    )(place, partners, *own_rows, *others)


def solved_sum(place_ref, partners_ref, row_refs, high_refs, low_refs):
    rounds = row_refs[0].shape[1] // SLOT
    first, second = 0.0, 0.0
    for turn in range(rounds):
        cells = slice(SLOT * turn, SLOT * turn + SLOT)
        high = jnp.concatenate([x[cells, :] for x in high_refs], axis=0)
        low = jnp.concatenate([x[cells, :] for x in low_refs], axis=0)
        solved = mul3(row_weights(row_refs, cells), (high, low), NN)
        listed = partners_ref[turn, place_ref[0]]
        first = first + jnp.where(listed == 0, solved, 0.0)
        second = second + jnp.where(listed == 1, solved, 0.0)
    return first, second


def near_kernel(place_ref, partners_ref, *refs):
    factor_ref, zero_ref, one_ref = refs[6:]
    first, second = solved_sum(place_ref, partners_ref, refs[:2], refs[2:4], refs[4:6])
    zero_ref[...] = jnp.where(place_ref[0] == 0, factor_ref[...], first)
    one_ref[...] = jnp.where(place_ref[0] == 1, factor_ref[...], second)


def far_kernel(place_ref, partners_ref, *refs):
    near_zero_ref, near_one_ref, zero_ref, one_ref = refs[6:]
    first, second = solved_sum(place_ref, partners_ref, refs[:2], refs[2:4], refs[4:6])
    zero_ref[...] = near_zero_ref[...] + jnp.where(place_ref[0] == 0, 0.0, first)
    one_ref[...] = near_one_ref[...] + jnp.where(place_ref[0] == 1, 0.0, second)


def chosen_sum(place_ref, partners_ref, row_refs, high_refs, low_refs):
    block = place_ref[0]
    later = partners_ref[1, block]
    is_later = jnp.logical_or(later == 0, later == 1)
    listed = jnp.where(is_later, later, partners_ref[0, block])
    pieces = []
    for ref in row_refs:
        quarter = ref.shape[0] - TRIPLE
        parts = []
        for turn in range(2):
            cells = slice(SLOT * turn, SLOT * turn + SLOT)
            parts.append(ref[:quarter, cells].astype(jnp.float32) * triple_sum(ref[quarter:, cells]))
        pieces.append(jnp.where(is_later, parts[1], parts[0]))
    weight = halves(jnp.concatenate(pieces, axis=1))
    high = jnp.concatenate([x[...] for x in high_refs], axis=0)
    low = jnp.concatenate([x[...] for x in low_refs], axis=0)
    solved = mul3(weight, (high, low), NN)
    return jnp.where(listed == 0, solved, 0.0), jnp.where(listed == 1, solved, 0.0)


def near_chosen_kernel(place_ref, partners_ref, *refs):
    factor_ref, zero_ref, one_ref = refs[6:]
    first, second = chosen_sum(place_ref, partners_ref, refs[:2], refs[2:4], refs[4:6])
    zero_ref[...] = jnp.where(place_ref[0] == 0, factor_ref[...], first)
    one_ref[...] = jnp.where(place_ref[0] == 1, factor_ref[...], second)


def far_chosen_kernel(place_ref, partners_ref, *refs):
    near_zero_ref, near_one_ref, zero_ref, one_ref = refs[6:]
    first, second = chosen_sum(place_ref, partners_ref, refs[:2], refs[2:4], refs[4:6])
    zero_ref[...] = near_zero_ref[...] + jnp.where(place_ref[0] == 0, 0.0, first)
    one_ref[...] = near_one_ref[...] + jnp.where(place_ref[0] == 1, 0.0, second)


def panels(kernel, place, partners, own_rows, highs, lows, more):
    shape = jax.ShapeDtypeStruct((own_rows[0].shape[0] - TRIPLE, highs[0].shape[1]), jnp.float32)
    return pl.pallas_call(
        kernel,
        out_shape=(shape, shape),
        in_specs=[SMEM, SMEM] + [VMEM] * (6 + len(more)),
        out_specs=(VMEM, VMEM),
        compiler_params=params(),
        cost_estimate=pl.CostEstimate(flops=3 * 10**9, bytes_accessed=5 * 10**6, transcendentals=0),
        name=kernel.__name__[:-7] + "_panels",
    )(place, partners, *own_rows, *highs, *lows, *more)


def spread(array, axis, root):
    mine = lax.axis_index(axis) == root
    return lax.psum(jnp.where(mine, array, jnp.zeros_like(array)), axis)


def exact_nt(left, right):
    return lax.dot_general(
        left, right, NT, precision=lax.Precision.HIGHEST, preferred_element_type=jnp.float32
    )


def coupled_panel(panel0, diag_part, tile_part, own_row, block_id, slab_id):
    quarter = panel0.shape[0]
    left_part, second_part = spread(panel0, "blk", 1), spread(diag_part, "blk", 1)
    left_full = lax.all_gather(left_part, "slab", axis=0, tiled=True)
    second_full = lax.all_gather(second_part, "slab", axis=0, tiled=True)
    second_factor = jnp.linalg.cholesky(second_full - exact_nt(left_full, left_full))
    col_second = jnp.sum(jnp.where((own_row == 1)[None, :, None], tile_part, 0.0), axis=1)
    rest = col_second - exact_nt(panel0, left_full)
    solved = jax.scipy.linalg.solve_triangular(second_factor, rest.T, lower=True).T
    second_rows = lax.dynamic_slice_in_dim(second_factor, slab_id * quarter, quarter, 0)
    return jnp.where(
        block_id == 0, jnp.zeros_like(solved), jnp.where(block_id == 1, second_rows, solved)
    )


def swap(array, step):
    return lax.ppermute(array, "slab", [(i, i ^ step) for i in range(lax.axis_size("slab"))])


def unscaled_halves(array):
    array = array.astype(jnp.float32) * (1.0 / SOLVE_SCALE)
    high = lax.reduce_precision(array, 8, 7)
    return high.astype(jnp.bfloat16), (array - high).astype(jnp.bfloat16)


def on_device(priv_coeff, priv_var, shared_coeff, shared_var, partners):
    rows = priv_coeff.shape[0]
    blocks, rounds = partners.shape
    block_id = lax.axis_index("blk").astype(jnp.int32)
    slab_id = lax.axis_index("slab").astype(jnp.int32)
    slabs = lax.axis_size("slab")
    quarter = rows // slabs
    place = jnp.stack([block_id, slab_id, slab_id % 2])
    table = partners.T

    pieces, *own_rows = pack(place, shared_coeff, shared_var, blocks, slabs)
    held = lax.all_to_all(pieces, "blk", 0, 0, tiled=True)
    own_rows = [swap(x, step) if step else x for step, x in enumerate(own_rows)]

    partial = partial_diag(place, priv_coeff, priv_var)
    partial, held, own_rows = lax.optimization_barrier((partial, held, own_rows))
    partial = add_shared(place, table, shared_coeff, shared_var, held, partial)
    up, down = DIAG_SCALE, 1.0 / DIAG_SCALE
    near = partial[0] + swap((partial[1] * up).astype(jnp.float16), 1).astype(jnp.float32) * down
    leaving, held = lax.optimization_barrier(((near * up).astype(jnp.float16), held))
    across = swap(leaving, 2)

    mate_coeff = lax.all_to_all(forward(table, held), "blk", 0, 0, tiled=True).reshape(rows, -1)
    cells = SLOT // blocks
    turned = shared_coeff.reshape(rows, rounds, blocks, cells).transpose(2, 1, 3, 0)
    turned = turned.reshape(rounds * SLOT, rows).astype(jnp.float32)
    across, mate_coeff, turned = lax.optimization_barrier((across, mate_coeff, turned))
    mine = near + across.astype(jnp.float32) * down

    from_zero, from_one = partners == 0, partners == 1
    one_each = jnp.logical_not(jnp.any(jnp.any(from_zero, axis=1) & jnp.any(from_one, axis=1)))
    is_coupled = jnp.any(from_zero[1])
    is_simple = one_each & jnp.logical_not(is_coupled)
    later = from_zero[:, 1] | from_one[:, 1]
    zero_later = jnp.where(later, from_zero[:, 1], from_zero[:, 0])
    choice = jnp.where(zero_later, 0, 2) + later.astype(jnp.int32)
    mine, choice, is_simple, is_coupled = lax.optimization_barrier((mine, choice, is_simple, is_coupled))

    other = swap(mine, 1)
    others = [swap(mate_coeff, step) if step else mate_coeff for step in (0, 1, 2)]
    factor_rows, solved = chol_solve(place, mine, other, turned, quarter)
    out = (solved * SOLVE_SCALE).astype(jnp.float16).reshape(blocks, rounds * cells, rows)
    spread_out = lax.all_to_all(out, "blk", 0, 0, tiled=True)
    diag_part = unpack_rows(place, mine, other, rows)
    _, others = lax.optimization_barrier((out, others))
    others = others + [swap(others[2], 1)]
    tile_part = pair_tiles(place, table, own_rows, others)
    spread_out, diag_part, tile_part = lax.optimization_barrier((spread_out, diag_part, tile_part))

    sources = [spread_out[i, cells * turn : cells * turn + cells] for i in (0, 1) for turn in (0, 1)]
    onward = jnp.broadcast_to(sources[0][None], (blocks, cells, rows))
    for number, source in enumerate(sources[1:], 1):
        onward = jnp.where((choice == number)[:, None, None], source[None], onward)
    arrived = lax.all_to_all(onward, "blk", 0, 0, tiled=True)
    tile_part = tile_part.reshape(quarter, rounds, rows)
    arrived, tile_part = lax.optimization_barrier((arrived, tile_part))

    def near_half(arrived, kernel):
        beside, across = swap(arrived, 1), swap(arrived, 2)
        highs, lows = zip(*[unscaled_halves(x) for x in (arrived, beside)])
        close = panels(kernel, place, table, own_rows[:2], highs, lows, (factor_rows,))
        across, close = lax.optimization_barrier((across, close))
        highs, lows = zip(*[unscaled_halves(x) for x in (across, swap(across, 1))])
        return highs, lows, close

    highs, lows, close = near_half(arrived.reshape(SLOT, rows), near_chosen_kernel)

    def simple():
        return panels(far_chosen_kernel, place, table, own_rows[2:], highs, lows, close)

    def general():
        wanted = jnp.repeat(from_zero, cells, axis=1)[:, :, None]
        both = jnp.where(wanted, spread_out[0][None], spread_out[1][None])
        both = lax.all_to_all(both, "blk", 0, 0, tiled=True).reshape(blocks, rounds, cells, rows)
        both = both.transpose(1, 0, 2, 3).reshape(solved.shape)
        highs, lows, close = near_half(both, near_kernel)
        panel0, panel1 = panels(far_kernel, place, table, own_rows[2:], highs, lows, close)
        own_row = lax.dynamic_index_in_dim(partners, block_id, 0, False)
        panel1 = lax.cond(
            is_coupled,
            lambda: coupled_panel(panel0, diag_part, tile_part, own_row, block_id, slab_id),
            lambda: panel1,
        )
        return panel0, panel1

    panel0, panel1 = lax.cond(is_simple, simple, general)
    return (diag_part[None], tile_part[None], panel0, panel1)


def solution(mesh):
    in_specs = (P("blk", "slab"), P("blk", "slab"), P("blk", "slab"), P("blk", "slab"), P())
    out_specs = (
        P("blk", "slab", None),
        P("blk", "slab", None, None),
        P(("blk", "slab"), None),
        P(("blk", "slab"), None),
    )
    return jax.shard_map(
        on_device, mesh=mesh, in_specs=in_specs, out_specs=out_specs, check_vma=False
    )
```
